256 devices in a mesh: seq: 32 (over y, x, core), tp: 8 (over z).
Axes of the slice: x: 4, y: 4, z: 8, core: 2. Of those that a mesh axis runs over, the one named last changes fastest.
Arguments:
- queries: bfloat16 [8192, 8192], P('seq', 'tp'), may hold values from -5 to 5
- teacher_keys: bfloat16 [8192, 1024], P('seq', 'tp'), may hold values from -5 to 5
- teacher_values: bfloat16 [8192, 1024], P('seq', 'tp'), may hold values from -6 to 6
- student_x: bfloat16 [8192, 8192], P('seq', 'tp'), may hold values from -0.59765625 to 0.59765625
- student_b: bfloat16 [8192, 128], P('seq'), may hold values from -2.09375 to 2.09375
- student_c: bfloat16 [8192, 8192], P('seq', 'tp'), may hold values from -0.29882812 to 0.29882812
- gate_input: bfloat16 [8192, 8192], P('seq', 'tp'), may hold values from -6 to 6
- step_rates: float32 [8192, 64], P('seq', 'tp'), may hold values from 0 to 1, as said below
- skip_gain: float32 [64], P('tp'), may hold values from 0.5 to 1.5
- doc_ids: int32 [8192], P('seq'), may hold values from 0 to 7, as said below
Outputs:
- grad_x: bfloat16 [8192, 8192], P('seq', 'tp')
- grad_b: bfloat16 [8192, 128], P(('seq', 'tp'))
- grad_c: bfloat16 [8192, 8192], P('seq', 'tp')
The draws below stay inside these ranges and needn't reach their ends.
Inputs may be any that keep to these rules, and one draw needn't show every extreme that they name: `step_rates`: positive. `doc_ids`: never falling; every document holds 1 to 4097 tokens; the one of exactly 4097 tokens begins 1 to 255 tokens after the first quarter of the 8192 tokens.
All inputs are finite; a program needn't handle non-finite values.
Results may differ from the reference program's by a relative error of at most 0.03.
Values may be sent and summed in bfloat16 or wider, within the bound.
A program may use at most 192 MiB of HBM per device.

```python
import math
import jax
import jax.numpy as jnp
from jax import lax

TOK_DEV = 256
ATTENDER_COUNT = 64
KV_HEADS = 8
HEAD_DIM = 128
STATE = 128
DOCS = 8
SEQUENCE_LENGTH = 8192
DOC_MOST = 4097


def draw_teacher_keys(key, part):
    key = jax.random.fold_in(key, 1)
    drawn_key, heavy_key = jax.random.split(key)
    row_shape = (SEQUENCE_LENGTH, KV_HEADS, HEAD_DIM)
    drawn_numbers = jax.random.truncated_normal(drawn_key, -5.0, 5.0, row_shape, jnp.float32)
    heavy_numbers = jax.random.truncated_normal(heavy_key, -2.0, 2.0, row_shape, jnp.float32) * 2.5
    heavy_rows = (jnp.arange(SEQUENCE_LENGTH) % TOK_DEV == TOK_DEV - 1)[:, None, None]
    drawn_numbers = jnp.where(heavy_rows, heavy_numbers, drawn_numbers)
    return drawn_numbers.reshape(SEQUENCE_LENGTH, KV_HEADS * HEAD_DIM).astype(jnp.bfloat16)


def draw_queries(key, part):
    key = jax.random.fold_in(key, 2)
    drawn_numbers = jax.random.truncated_normal(key, -5.0, 5.0, (SEQUENCE_LENGTH, ATTENDER_COUNT, HEAD_DIM), jnp.float32)
    return drawn_numbers.reshape(SEQUENCE_LENGTH, ATTENDER_COUNT * HEAD_DIM).astype(jnp.bfloat16)


def draw_step_rates(key, part):
    key = jax.random.fold_in(key, 3)
    attender_seed, quick_decay_seed, spread_seed, device_noise_seed, noise_seed, spike_seed, length_seed = jax.random.split(key, 7)
    lower_rate = 0.2 / SEQUENCE_LENGTH
    fast_share = 0.2
    upper_rate = 1.0 / 30.0
    fast_heads = jax.random.bernoulli(attender_seed, fast_share, (ATTENDER_COUNT,))
    fast_rate = jax.random.uniform(quick_decay_seed, (ATTENDER_COUNT,), jnp.float32, 1.0 / 50.0, 1.0 / 30.0)
    spread_rate = jnp.exp(jax.random.uniform(spread_seed, (ATTENDER_COUNT,), jnp.float32, math.log(lower_rate), math.log(upper_rate)))
    resting_decay = jnp.where(fast_heads, fast_rate, spread_rate)
    channel_factor = jnp.exp(jax.random.uniform(device_noise_seed, (SEQUENCE_LENGTH // TOK_DEV, 1), jnp.float32, -0.4, 0.4))
    channel_factor = jnp.repeat(channel_factor, TOK_DEV, axis=0)
    noise_spread = jax.random.uniform(noise_seed, (SEQUENCE_LENGTH, ATTENDER_COUNT), jnp.float32, 0.5, 1.5)
    spike_location = jax.random.randint(spike_seed, (3,), 0, SEQUENCE_LENGTH)
    spike_present = jnp.any(jnp.arange(SEQUENCE_LENGTH)[:, None] == spike_location[None, :], axis=1)
    spike_strength = jax.random.uniform(length_seed, (SEQUENCE_LENGTH, ATTENDER_COUNT), jnp.float32, 0.22, 0.69)
    drawn_numbers = resting_decay[None, :] * channel_factor * noise_spread + jnp.where(spike_present[:, None], spike_strength, 0.0)
    return drawn_numbers.astype(jnp.float32)


def draw_doc_ids(key, part):
    key = jax.random.fold_in(key, 4)
    start_key, order_key = jax.random.split(key)
    offset = jax.random.randint(start_key, (), 1, TOK_DEV).astype(jnp.int32)
    long_start = (SEQUENCE_LENGTH // 4 + offset).astype(jnp.int32)
    long_stop = (long_start + DOC_MOST).astype(jnp.int32)
    places = jnp.arange(SEQUENCE_LENGTH, dtype=jnp.int32)
    ranking = jax.random.permutation(order_key, SEQUENCE_LENGTH).astype(jnp.int32)
    eligible = (places >= 1) & (places < long_start) | (places > long_stop)
    masked = jnp.where(eligible, ranking, -1)
    picked_scores, picked = lax.top_k(masked, DOCS - 3)
    cuts = jnp.concatenate([picked.astype(jnp.int32), jnp.stack([long_start, long_stop]).astype(jnp.int32)])
    return jnp.sum((places[:, None] >= cuts[None, :]).astype(jnp.int32), axis=1).astype(jnp.int32)


def levels(own_key, shape, cuts, smallest, top_value):
    def one(axis_at, blocks):
        heights = jax.random.uniform(jax.random.fold_in(jax.random.fold_in(own_key, 6), axis_at), (blocks,), jnp.float32, smallest / len(cuts), top_value / len(cuts))
        return jnp.repeat(jnp.exp(heights), shape[axis_at] // blocks).reshape((-1,) + (1,) * (len(shape) - axis_at - 1))

    loudness = one(*cuts[0])
    for cut in cuts[1:]:
        loudness = loudness * one(*cut)
    return loudness


def noise(stream_key, shape, deviation, most, cuts=(), kind=jnp.bfloat16):
    loudness = levels(stream_key, shape, cuts, -0.22, 0.18) if cuts else 1.0
    values = jax.random.normal(stream_key, shape, jnp.float32) * deviation * loudness
    return jnp.minimum(jnp.maximum(values, -most), most).astype(kind)


def setup_inputs(seed: int = 0) -> dict:
    arg_keys = jax.random.split(jax.random.key(seed), 11)
    return {
        "queries": draw_queries(jax.random.fold_in(arg_keys[10], 71), 0),
        "teacher_keys": draw_teacher_keys(jax.random.fold_in(arg_keys[10], 71), 0),
        "teacher_values": noise(arg_keys[2], (SEQUENCE_LENGTH, KV_HEADS * HEAD_DIM), 1.0, 6.0, ((0, 32), (1, 8))),
        "student_x": noise(arg_keys[3], (SEQUENCE_LENGTH, ATTENDER_COUNT * HEAD_DIM), 0.1, 0.59765625, ((0, 32), (1, 8))),
        "student_b": noise(arg_keys[4], (SEQUENCE_LENGTH, STATE), 0.35, 2.09375, ((0, 32),)),
        "student_c": noise(arg_keys[5], (SEQUENCE_LENGTH, ATTENDER_COUNT * STATE), 0.05, 0.29882812, ((0, 32), (1, 8))),
        "gate_input": noise(arg_keys[6], (SEQUENCE_LENGTH, ATTENDER_COUNT * HEAD_DIM), 1.0, 6.0, ((0, 32), (1, 8))),
        "step_rates": draw_step_rates(jax.random.fold_in(arg_keys[10], 71), 0),
        "skip_gain": jnp.clip(0.5 + 1.0 * jax.random.uniform(arg_keys[8], (ATTENDER_COUNT,), jnp.float32) ** levels(arg_keys[8], (ATTENDER_COUNT,), ((0, 8),), -0.2, 0.2), 0.5, 1.5),
        "doc_ids": draw_doc_ids(jax.random.fold_in(arg_keys[10], 71), 0),
    }


def contract(pattern, first_arg, second_arg):
    return jnp.einsum(pattern, first_arg.astype(jnp.float32), second_arg.astype(jnp.float32), precision=lax.Precision.HIGHEST)

def decay_table(block_ids, step_rates):
    log_decay = jnp.cumsum(-step_rates, axis=0)
    length = block_ids.shape[0]
    places = jnp.arange(length, dtype=jnp.int32)
    linked = (block_ids[:, None] == block_ids[None, :]) & (places[:, None] >= places[None, :])
    spread = log_decay.T[:, :, None] - log_decay.T[:, None, :]
    decays = jnp.where(linked[None], jnp.exp(jnp.where(linked[None], spread, 0.0)), 0.0)
    return (log_decay, decays)

def block_through(block_ids, log_decay):
    return jnp.where(block_ids[0] == block_ids[-1], jnp.exp(log_decay[-1]), 0.0)

def forward_combine(earlier, later):
    first_a, last_a, through_a, state_a = earlier
    first_b, last_b, through_b, state_b = later
    linked = ((last_a == first_b) | (last_a < 0) | (first_b < 0)).astype(jnp.float32)
    passing = through_b * linked
    return (jnp.where(first_a < 0, first_b, first_a), jnp.where(last_b < 0, last_a, last_b), through_a * passing, passing[:, None, None] * state_a + state_b)

def reverse_combine(higher, lower):
    first_h, last_h, through_h, state_h = higher
    first_l, last_l, through_l, state_l = lower
    linked = ((last_l == first_h) | (last_l < 0) | (first_h < 0)).astype(jnp.float32)
    passing = through_l * linked
    return (jnp.where(first_l < 0, first_h, first_l), jnp.where(last_h < 0, last_l, last_h), through_h * passing, state_l + passing[:, None, None] * state_h)

def chain_identity(head_count):
    missing = -jnp.ones((), jnp.int32)
    return (missing, missing, jnp.ones((head_count,), jnp.float32), jnp.zeros((head_count, STATE, HEAD_DIM), jnp.float32))

def chain_element(block_ids, log_decay, student_b, x_heads):
    end_weights = jnp.where((block_ids == block_ids[-1])[:, None], jnp.exp(log_decay[-1][None, :] - log_decay), 0.0)
    weighted = (student_b[:, None, :].astype(jnp.float32) * end_weights[:, :, None]).astype(jnp.bfloat16)
    block_state = contract('thn,thp->hnp', weighted, x_heads)
    return (block_ids[0], block_ids[-1], block_through(block_ids, log_decay), block_state)

def forward_delta(block_ids, log_decay, mixing, c_heads, x_heads, gate_heads, teacher, skip_gain, last_in, state_in):
    inner_part = contract('hst,thp->shp', mixing, x_heads)
    carried = jnp.where((block_ids == last_in)[:, None], jnp.exp(log_decay), 0.0)
    state_low = state_in.astype(jnp.bfloat16)
    carried_part = contract('shn,hnp->shp', c_heads, state_low) * carried[:, :, None]
    studied = inner_part + carried_part + skip_gain[None, :, None] * x_heads.astype(jnp.float32)
    opened = jax.nn.silu(gate_heads.astype(jnp.float32))
    mismatch = studied * opened - teacher.astype(jnp.float32)
    grad_y = (mismatch * opened).astype(jnp.bfloat16)
    return (carried, state_low, grad_y)

def reverse_element(block_ids, log_decay, c_heads, grad_y):
    starts = jnp.where((block_ids == block_ids[0])[:, None], jnp.exp(log_decay), 0.0)
    weighted = (c_heads.astype(jnp.float32) * starts[:, :, None]).astype(jnp.bfloat16)
    block_grad = contract('shn,shp->hnp', weighted, grad_y)
    return (block_ids[0], block_ids[-1], block_through(block_ids, log_decay), block_grad)

def backward(block_ids, log_decay, decays, mixing, student_b, c_heads, x_heads, grad_y, carried, state_low, skip_gain, first_out, grad_in):
    to_next = jnp.where((block_ids == first_out)[:, None], jnp.exp(log_decay[-1][None, :] - log_decay), 0.0)
    grad_low = grad_in.astype(jnp.bfloat16)
    grad_x = contract('hst,shp->thp', mixing, grad_y) + contract('tn,hnp->thp', student_b, grad_low) * to_next[:, :, None] + skip_gain[None, :, None] * grad_y.astype(jnp.float32)
    grad_mixing = (contract('shp,thp->hst', grad_y, x_heads) * decays).astype(jnp.bfloat16)
    grad_c = contract('hst,tn->shn', grad_mixing, student_b) + contract('shp,hnp->shn', grad_y, state_low) * carried[:, :, None]
    head_terms = contract('hst,shn->tn', grad_mixing, c_heads) + lax.optimization_barrier(jnp.sum(contract('thp,hnp->thn', x_heads, grad_low) * to_next[:, :, None], axis=1))
    return (grad_x.astype(jnp.bfloat16), grad_c.astype(jnp.bfloat16), head_terms)

def teacher_attention(queries, teacher_keys, teacher_values, doc_ids):
    groups = ATTENDER_COUNT // KV_HEADS
    blocks = SEQUENCE_LENGTH // TOK_DEV
    key_heads = teacher_keys.reshape(SEQUENCE_LENGTH, KV_HEADS, HEAD_DIM)
    value_heads = teacher_values.reshape(SEQUENCE_LENGTH, KV_HEADS, HEAD_DIM)
    places = jnp.arange(SEQUENCE_LENGTH, dtype=jnp.int32)
    query_blocks = queries.reshape(blocks, TOK_DEV, KV_HEADS, groups, HEAD_DIM)
    id_blocks = doc_ids.reshape(blocks, TOK_DEV)
    pos_blocks = places.reshape(blocks, TOK_DEV)

    def one_block(block_item):
        grouped, block_ids, query_pos = block_item
        allowed = ((block_ids[:, None] == doc_ids[None, :]) & (query_pos[:, None] >= places[None, :]))[:, None, None, :]
        scores = contract('tkgp,skp->tkgs', grouped, key_heads) * (1.0 / math.sqrt(HEAD_DIM))
        scores = jnp.where(allowed, scores, -1e+30)
        highest = lax.optimization_barrier(jnp.max(scores, axis=3, keepdims=True))
        weights = jnp.where(allowed, jnp.exp(scores - highest), 0.0)
        weight_sum = lax.optimization_barrier(jnp.sum(weights, axis=3))
        mixed = contract('tkgs,skp->tkgp', weights.astype(jnp.bfloat16), value_heads)
        return (mixed / weight_sum[..., None]).astype(jnp.bfloat16)
    return lax.map(one_block, (query_blocks, id_blocks, pos_blocks))

def reference(queries, teacher_keys, teacher_values, student_x, student_b, student_c, gate_input, step_rates, skip_gain, doc_ids):
    blocks = SEQUENCE_LENGTH // TOK_DEV
    teacher = teacher_attention(queries, teacher_keys, teacher_values, doc_ids).reshape(blocks, TOK_DEV, ATTENDER_COUNT, HEAD_DIM)
    id_blocks = doc_ids.reshape(blocks, TOK_DEV)
    rate_blocks = step_rates.reshape(blocks, TOK_DEV, ATTENDER_COUNT)
    b_blocks = student_b.reshape(blocks, TOK_DEV, STATE)
    c_blocks = student_c.reshape(blocks, TOK_DEV, ATTENDER_COUNT, STATE)
    x_blocks = student_x.reshape(blocks, TOK_DEV, ATTENDER_COUNT, HEAD_DIM)
    gate_blocks = gate_input.reshape(blocks, TOK_DEV, ATTENDER_COUNT, HEAD_DIM)

    def first_pass(block_item):
        block_ids, rates_here, b_here, x_here = block_item
        log_decay, decays = decay_table(block_ids, rates_here)
        return chain_element(block_ids, log_decay, b_here, x_here)
    elements = lax.map(first_pass, (id_blocks, rate_blocks, b_blocks, x_blocks))

    def forward_step(folded, element):
        return (forward_combine(folded, element), folded)
    ignored, incoming = lax.scan(forward_step, chain_identity(ATTENDER_COUNT), elements)

    def second_pass(block_item):
        block_ids, rates_here, b_here, c_here, x_here, gate_here, teacher_here, last_in, state_in = block_item
        log_decay, decays = decay_table(block_ids, rates_here)
        mixing = (contract('shn,tn->hst', c_here, b_here) * decays).astype(jnp.bfloat16)
        carried, state_low, grad_y = forward_delta(block_ids, log_decay, mixing, c_here, x_here, gate_here, teacher_here, skip_gain, last_in, state_in)
        return reverse_element(block_ids, log_decay, c_here, grad_y)
    back_elements = lax.map(second_pass, (id_blocks, rate_blocks, b_blocks, c_blocks, x_blocks, gate_blocks, teacher, incoming[1], incoming[3]))

    def reverse_step(folded, element):
        return (reverse_combine(folded, element), folded)
    ignored, outgoing = lax.scan(reverse_step, chain_identity(ATTENDER_COUNT), back_elements, reverse=True)

    def third_pass(block_item):
        block_ids, rates_here, b_here, c_here, x_here, gate_here, teacher_here, last_in, state_in, first_out, grad_in = block_item
        log_decay, decays = decay_table(block_ids, rates_here)
        mixing = (contract('shn,tn->hst', c_here, b_here) * decays).astype(jnp.bfloat16)
        carried, state_low, grad_y = forward_delta(block_ids, log_decay, mixing, c_here, x_here, gate_here, teacher_here, skip_gain, last_in, state_in)
        grad_x, grad_c, head_terms = backward(block_ids, log_decay, decays, mixing, b_here, c_here, x_here, grad_y, carried, state_low, skip_gain, first_out, grad_in)
        return (grad_x, grad_c, head_terms.astype(jnp.bfloat16))
    grad_x, grad_c, grad_b = lax.map(third_pass, (id_blocks, rate_blocks, b_blocks, c_blocks, x_blocks, gate_blocks, teacher, incoming[1], incoming[3], outgoing[0], outgoing[3]))
    return (grad_x.reshape(SEQUENCE_LENGTH, ATTENDER_COUNT * HEAD_DIM), grad_b.reshape(SEQUENCE_LENGTH, STATE), grad_c.reshape(SEQUENCE_LENGTH, ATTENDER_COUNT * STATE))
```

```python
import functools
import math

import jax
import jax.numpy as jnp
from jax import lax
from jax.experimental import pallas as pl
from jax.experimental.pallas import tpu as pltpu
from jax.sharding import PartitionSpec as P

MESH = pl.DeviceIdType.MESH
F32 = jnp.float32
BF16 = jnp.bfloat16

T = 256
H = 8
D = 128
FEAT = 16
KROWS = D + FEAT
FAR = 16
CHUNK = 4
PIECES = 32
PER = PIECES // H
PROWS = D // PER
META = 16
BIG = 1e30
LOG2E = math.log2(math.e)
SCALE2 = LOG2E / math.sqrt(D)


def dot(a, b):
    return lax.dot_general(a, b, (((1,), (0,)), ((), ())), preferred_element_type=F32)


def dot_t(a, b):
    return lax.dot_general(a, b, (((1,), (1,)), ((), ())), preferred_element_type=F32)


def head_lanes(h):
    return pl.ds(pl.multiple_of(h * D, D), D)


def wide(a, n):
    return jnp.concatenate([a] * n, axis=1)


def kernel(
    ids_ref,
    rates_ref,
    skip_ref,
    q_ref,
    k_ref,
    v_ref,
    x_ref,
    b_ref,
    c_ref,
    gate_ref,
    gx_ref,
    gb_ref,
    gc_ref,
    own_k,
    own_v,
    far_k,
    far_v,
    qp,
    acc,
    top,
    log_row,
    log_col,
    mask,
    mask_t,
    decay,
    decay_t,
    mix_t,
    wc_t,
    b_t,
    ids_col,
    inner,
    g_ref,
    gx_part,
    h_term,
    state_send,
    state_recv,
    entry_send,
    entry_recv,
    grad_send,
    grad_recv,
    exit_send,
    exit_recv,
    tp_send,
    tp_recv,
    kv_send_sem,
    kv_recv_sem,
    send_sem,
    recv_sem,
):
    me = lax.axis_index("seq")
    z = lax.axis_index("tp")
    n_seq, n_tp = PIECES, 8

    def clear(j, carry):
        at = pl.ds(pl.multiple_of(j * T, T), T)
        far_k[0:D, at] = jnp.zeros((D, T), BF16)
        far_k[D:KROWS, at] = jnp.full((FEAT, T), -BIG, BF16)
        far_k[KROWS:, at] = jnp.zeros((T - KROWS, T), BF16)
        far_v[at, 0:D] = jnp.zeros((T, D), BF16)
        far_v[at, D:] = jnp.ones((T, D), BF16)
        return carry

    lax.fori_loop(0, FAR, clear, 0)

    barrier = pltpu.get_barrier_semaphore()

    def greet_seq(k, carry):
        pl.semaphore_signal(
            barrier, inc=1, device_id=(lax.rem(me + k, n_seq), z), device_id_type=MESH
        )
        return carry

    def greet_tp(k, carry):
        pl.semaphore_signal(
            barrier, inc=1, device_id=(me, lax.rem(z + k, n_tp)), device_id_type=MESH
        )
        return carry

    lax.fori_loop(1, n_seq, greet_seq, 0)
    lax.fori_loop(1, n_tp, greet_tp, 0)

    ids_row = ids_ref[...].astype(F32)
    first_id = ids_row[:, 0:1]
    last_id = ids_row[:, T - 1 : T]
    feat_row = lax.broadcasted_iota(jnp.int32, (FEAT, T), 0).astype(F32)
    own_k[0:D, :] = k_ref[...].astype(F32).T.astype(BF16)
    own_k[D:KROWS, :] = jnp.where(
        feat_row == jnp.broadcast_to(ids_row, (FEAT, T)), 0.0, -BIG
    ).astype(BF16)
    own_k[KROWS:, :] = jnp.zeros((T - KROWS, T), BF16)
    own_v[:, 0:D] = v_ref[...]
    own_v[:, D:] = jnp.ones((T, D), BF16)
    b_t[...] = b_ref[...].astype(F32).T.astype(BF16)
    idc = jnp.broadcast_to(ids_row, (D, T)).T
    ids_col[...] = idc

    row = lax.broadcasted_iota(jnp.int32, (T, T), 0)
    col = lax.broadcasted_iota(jnp.int32, (T, T), 1)
    log_row[...] = -LOG2E * lax.dot_general(
        rates_ref[...],
        (row <= col).astype(F32),
        (((1,), (0,)), ((), ())),
        precision=lax.Precision.HIGHEST,
        preferred_element_type=F32,
    )
    same = wide(idc, 2) == jnp.broadcast_to(ids_row, (T, T))
    mask[...] = jnp.where(same & (row >= col), 0.0, -BIG)
    mask_t[...] = jnp.where(same & (row <= col), 0.0, -BIG)

    end_bias = jnp.where(ids_row == last_id, 0.0, -BIG)
    whole = jnp.where(first_id == last_id, 1.0, 0.0)
    meta_row = lax.broadcasted_iota(jnp.int32, (META, D), 0)

    def states(h, carry):
        lr = log_row[pl.ds(h, 1), :]
        lend = lr[:, T - 1 : T]
        weight = jnp.exp2(lend - lr + end_bias)
        wt = (b_t[...].astype(F32) * jnp.broadcast_to(weight, (D, T))).astype(BF16)
        st = dot(wt, x_ref[:, head_lanes(h)]).astype(BF16)
        thr = jnp.broadcast_to(jnp.exp2(lend) * whole, (META, D))
        high = thr.astype(BF16).astype(F32)
        meta = jnp.where(
            meta_row == 0,
            high,
            jnp.where(
                meta_row == 1,
                thr - high,
                jnp.where(
                    meta_row == 2,
                    jnp.broadcast_to(first_id, (META, D)),
                    jnp.broadcast_to(last_id, (META, D)),
                ),
            ),
        ).astype(BF16)
        for p in range(PER):
            state_send[h * PER + p, 0:PROWS, :] = st[p * PROWS : (p + 1) * PROWS, :]
            state_send[h * PER + p, PROWS:, :] = meta
        return carry

    lax.fori_loop(0, H, states, 0)

    pl.semaphore_wait(barrier, n_seq - 1 + n_tp - 1)

    def scatter(source, target, slot, peer):
        return pltpu.make_async_remote_copy(
            src_ref=source.at[peer],
            dst_ref=target.at[me],
            send_sem=send_sem.at[slot],
            recv_sem=recv_sem.at[slot],
            device_id=(peer, z),
            device_id_type=MESH,
        )

    def scatter_all(source, target, slot):
        def one(k, carry):
            scatter(source, target, slot, lax.rem(me + k, n_seq)).start()
            return carry

        lax.fori_loop(1, n_seq, one, 0)
        target[me] = source[me]

    def arrived(target, slot):
        rest = target.at[pl.ds(0, n_seq - 1)]
        pltpu.make_async_copy(rest, rest, recv_sem.at[slot]).wait()

    def left(source, slot):
        rest = source.at[pl.ds(0, n_seq - 1)]
        pltpu.make_async_copy(rest, rest, send_sem.at[slot]).wait()

    scatter_all(state_send, state_recv, 0)

    n_out = jnp.where(me < 8, 8 - me, jnp.where(me < 24, 24 - me, 31 - me))
    n_in = jnp.where(me <= 8, me, jnp.where(me <= 24, me - 8, me - 24))

    def kv_copies(d):
        at = pl.ds(pl.multiple_of(d * T, T), T)
        peer = lax.rem(me + 1 + d, n_seq)
        return (
            pltpu.make_async_remote_copy(
                src_ref=own_k.at[0:KROWS, :],
                dst_ref=far_k.at[0:KROWS, at],
                send_sem=kv_send_sem.at[0, d],
                recv_sem=kv_recv_sem.at[0, d],
                device_id=(peer, z),
                device_id_type=MESH,
            ),
            pltpu.make_async_remote_copy(
                src_ref=own_v.at[:, 0:D],
                dst_ref=far_v.at[at, 0:D],
                send_sem=kv_send_sem.at[1, d],
                recv_sem=kv_recv_sem.at[1, d],
                device_id=(peer, z),
                device_id_type=MESH,
            ),
        )

    def kv_start(d, carry):
        for copy in kv_copies(d):
            copy.start()
        return carry

    lax.fori_loop(0, n_out, kv_start, 0)

    first_bias = jnp.where(ids_row == first_id, 0.0, -BIG)
    lane = lax.broadcasted_iota(jnp.int32, (T, D), 1).astype(F32)
    q_feat = jnp.where(lane == idc, 1.0, 0.0).astype(BF16)

    def local(h, carry):
        lanes = head_lanes(h)
        lr = log_row[pl.ds(h, 1), :]
        lc = jnp.broadcast_to(lr, (D, T)).T
        log_col[h] = lc
        lrb = jnp.broadcast_to(lr, (T, T))
        lcb = wide(lc, 2)
        ch = c_ref[:, lanes]
        ct = ch.astype(F32).T
        xh = x_ref[:, lanes]
        dec = jnp.exp2(lcb - lrb + mask[...])
        decay[h] = dec
        mix = (dot(ch, b_t[...]) * dec).astype(BF16)
        inner[h] = dot(mix, xh) + skip_ref[h] * xh.astype(F32)
        dec_t = jnp.exp2(lrb - lcb + mask_t[...])
        decay_t[h] = dec_t
        mix_t[h] = (dot(b_ref[...], ct.astype(BF16)) * dec_t).astype(BF16)
        wc_t[h] = (ct * jnp.broadcast_to(jnp.exp2(lr + first_bias), (D, T))).astype(BF16)
        qh = jnp.concatenate([q_ref[:, lanes], q_feat], axis=1)
        qp[h] = qh
        s = jnp.where(row >= col, dot(qh, own_k[...]), -BIG)
        m = jnp.broadcast_to(jnp.max(s, axis=1, keepdims=True), (T, D))
        p = jnp.exp2((s - wide(m, 2)) * SCALE2)
        top[h] = m
        acc[h] = dot(p.astype(BF16), own_v[...])
        return carry

    lax.fori_loop(0, H, local, 0)

    arrived(state_recv, 0)

    def piece(c):
        got = state_recv[c]
        return got[PROWS : PROWS + 4, :].astype(F32)

    def forward(c, carry):
        total, last = carry
        got = state_recv[c].astype(F32)
        meta = got[PROWS:, :]
        entry_send[c, 0:PROWS, :] = total.astype(BF16)
        nxt = state_recv[jnp.minimum(c + 1, n_seq - 1), PROWS:, :].astype(F32)[2:3, :]
        nxt = jnp.where(c == n_seq - 1, -1.0, nxt)
        entry_send[c, PROWS:, :] = jnp.where(
            meta_row == 0,
            jnp.broadcast_to(last, (META, D)),
            jnp.broadcast_to(nxt, (META, D)),
        ).astype(BF16)
        passing = jnp.where(last == meta[2:3, :], meta[0:1, :] + meta[1:2, :], 0.0)
        return (jnp.broadcast_to(passing, (PROWS, D)) * total + got[0:PROWS, :], meta[3:4, :])

    lax.fori_loop(
        0, n_seq, forward, (jnp.zeros((PROWS, D), F32), jnp.full((1, D), -1.0, F32))
    )
    scatter_all(entry_send, entry_recv, 1)

    def attend(step):
        at = pl.ds(step * CHUNK * T, CHUNK * T)

        def head(h, carry):
            s = dot(qp[h], far_k[:, at])
            old = top[h]
            new = jnp.maximum(
                old, jnp.broadcast_to(jnp.max(s, axis=1, keepdims=True), (T, D))
            )
            p = jnp.exp2((s - wide(new, CHUNK * 2)) * SCALE2)
            shrink = jnp.exp2((old - new) * SCALE2)
            top[h] = new
            acc[h] = acc[h] * wide(shrink, 2) + dot(p.astype(BF16), far_v[at, :])
            return carry

        lax.fori_loop(0, H, head, 0)

    def kv_wait(d, carry):
        for copy in kv_copies(d):
            copy.wait_recv()
        return carry

    for step in range(FAR // CHUNK):
        lax.fori_loop(
            jnp.minimum(n_in, step * CHUNK),
            jnp.minimum(n_in, (step + 1) * CHUNK),
            kv_wait,
            0,
        )

        @pl.when(n_in > step * CHUNK)
        def _(step=step):
            attend(step)

    arrived(entry_recv, 1)
    ids_near = entry_recv[0, PROWS:, :].astype(F32)
    in_bias = jnp.where(idc == jnp.broadcast_to(ids_near[0:1, :], (T, D)), 0.0, -BIG)
    out_bias = jnp.where(idc == jnp.broadcast_to(ids_near[1:2, :], (T, D)), 0.0, -BIG)

    def state_of(ref, h):
        parts = [ref[h * PER + p, 0:PROWS, :] for p in range(PER)]
        return jnp.concatenate(parts, axis=0)

    def mismatch(h, carry):
        lanes = head_lanes(h)
        carried = jnp.exp2(log_col[h] + in_bias)
        studied = inner[h] + dot(c_ref[:, lanes], state_of(entry_recv, h)) * carried
        gate = gate_ref[:, lanes].astype(F32)
        opened = gate / (1.0 + jnp.exp(-gate))
        a = acc[h]
        teacher = (a[:, 0:D] / a[:, D:]).astype(BF16).astype(F32)
        g = ((studied * opened - teacher) * opened).astype(BF16)
        g_ref[h] = g
        bg = dot(wc_t[h], g).astype(BF16)
        for p in range(PER):
            to = h * PER + p
            grad_send[to] = bg[p * PROWS : (p + 1) * PROWS, :]

            @pl.when(to != me)
            def _():
                scatter(grad_send, grad_recv, 2, to).start()

        return carry

    lax.fori_loop(0, H, mismatch, 0)
    grad_recv[me] = grad_send[me]

    h_term[...] = jnp.zeros((T, D), F32)

    def within(h, carry):
        lanes = head_lanes(h)
        g = g_ref[h]
        xh = x_ref[:, lanes]
        gx_part[h] = dot(mix_t[h], g) + skip_ref[h] * g.astype(F32)
        gm = (dot_t(g, xh) * decay[h]).astype(BF16)
        carried = jnp.exp2(log_col[h] + in_bias)
        gc = dot(gm, b_ref[...]) + dot_t(g, state_of(entry_recv, h)) * carried
        gc_ref[:, lanes] = gc.astype(BF16)
        gm_t = (dot_t(xh, g) * decay_t[h]).astype(BF16)
        h_term[...] += dot(gm_t, c_ref[:, lanes])
        return carry

    lax.fori_loop(0, H // 2, within, 0)

    arrived(grad_recv, 2)

    def reverse(k, carry):
        total, nxt = carry
        c = n_seq - 1 - k
        meta = state_recv[c, PROWS:, :].astype(F32)
        exit_send[c] = total.astype(BF16)
        passing = jnp.where(nxt == meta[3:4, :], meta[0:1, :] + meta[1:2, :], 0.0)
        total = jnp.broadcast_to(passing, (PROWS, D)) * total + grad_recv[c].astype(F32)
        return (total, meta[2:3, :])

    lax.fori_loop(
        0, n_seq, reverse, (jnp.zeros((PROWS, D), F32), jnp.full((1, D), -1.0, F32))
    )
    scatter_all(exit_send, exit_recv, 3)

    lax.fori_loop(H // 2, H, within, 0)

    arrived(exit_recv, 3)

    def finish(h, carry):
        lanes = head_lanes(h)
        lc = log_col[h]
        to_next = jnp.exp2(jnp.broadcast_to(lc[T - 1 : T, :], (T, D)) - lc + out_bias)
        low = state_of(exit_recv, h)
        gx_ref[:, lanes] = (gx_part[h] + dot(b_ref[...], low) * to_next).astype(BF16)
        h_term[...] += dot_t(x_ref[:, lanes], low) * to_next
        return carry

    lax.fori_loop(0, H, finish, 0)

    rows = T // n_tp
    tp_send[...] = h_term[...].astype(BF16).reshape(n_tp, rows, D)

    def tp_copy(k, carry):
        peer = lax.rem(z + k, n_tp)
        pltpu.make_async_remote_copy(
            src_ref=tp_send.at[peer],
            dst_ref=tp_recv.at[z],
            send_sem=send_sem.at[4],
            recv_sem=recv_sem.at[4],
            device_id=(me, peer),
            device_id_type=MESH,
        ).start()
        return carry

    lax.fori_loop(1, n_tp, tp_copy, 0)
    tp_recv[z] = tp_send[z]
    rest = tp_recv.at[pl.ds(0, n_tp - 1)]
    pltpu.make_async_copy(rest, rest, recv_sem.at[4]).wait()
    total = jnp.zeros((rows, D), F32)
    for k in range(n_tp):
        total = total + tp_recv[k].astype(F32)
    gb_ref[...] = total.astype(BF16)

    left(state_send, 0)
    left(entry_send, 1)
    left(grad_send, 2)
    left(exit_send, 3)
    rest = tp_send.at[pl.ds(0, n_tp - 1)]
    pltpu.make_async_copy(rest, rest, send_sem.at[4]).wait()

    def kv_left(d, carry):
        for copy in kv_copies(d):
            copy.wait_send()
        return carry

    lax.fori_loop(0, n_out, kv_left, 0)


def shards(q, k, v, x, b, c, gate, rates, skip, ids):
    vmem = pl.BlockSpec(memory_space=pltpu.VMEM)
    smem = pl.BlockSpec(memory_space=pltpu.SMEM)
    return pl.pallas_call(
        kernel,
        out_shape=(
            jax.ShapeDtypeStruct((T, H * D), BF16),
            jax.ShapeDtypeStruct((T // 8, D), BF16),
            jax.ShapeDtypeStruct((T, H * D), BF16),
        ),
        in_specs=[vmem, vmem, smem] + [vmem] * 7,
        out_specs=(vmem, vmem, vmem),
        scratch_shapes=[
            pltpu.VMEM((T, T), BF16),
            pltpu.VMEM((T, T), BF16),
            pltpu.VMEM((T, FAR * T), BF16),
            pltpu.VMEM((FAR * T, T), BF16),
            pltpu.VMEM((H, T, T), BF16),
            pltpu.VMEM((H, T, T), F32),
            pltpu.VMEM((H, T, D), F32),
            pltpu.VMEM((H, T), F32),
            pltpu.VMEM((H, T, D), F32),
            pltpu.VMEM((T, T), F32),
            pltpu.VMEM((T, T), F32),
            pltpu.VMEM((H, T, T), F32),
            pltpu.VMEM((H, T, T), F32),
            pltpu.VMEM((H, T, T), BF16),
            pltpu.VMEM((H, D, T), BF16),
            pltpu.VMEM((D, T), BF16),
            pltpu.VMEM((T, D), F32),
            pltpu.VMEM((H, T, D), F32),
            pltpu.VMEM((H, T, D), BF16),
            pltpu.VMEM((H, T, D), F32),
            pltpu.VMEM((T, D), F32),
            pltpu.VMEM((PIECES, PROWS + META, D), BF16),
            pltpu.VMEM((PIECES, PROWS + META, D), BF16),
            pltpu.VMEM((PIECES, PROWS + META, D), BF16),
            pltpu.VMEM((PIECES, PROWS + META, D), BF16),
            pltpu.VMEM((PIECES, PROWS, D), BF16),
            pltpu.VMEM((PIECES, PROWS, D), BF16),
            pltpu.VMEM((PIECES, PROWS, D), BF16),
            pltpu.VMEM((PIECES, PROWS, D), BF16),
            pltpu.VMEM((8, T // 8, D), BF16),
            pltpu.VMEM((8, T // 8, D), BF16),
            pltpu.SemaphoreType.DMA((2, FAR)),
            pltpu.SemaphoreType.DMA((2, FAR)),
            pltpu.SemaphoreType.DMA((5,)),
            pltpu.SemaphoreType.DMA((5,)),
        ],
        compiler_params=pltpu.CompilerParams(
            collective_id=0, has_side_effects=True, vmem_limit_bytes=56 * 1024 * 1024
        ),
        name="distill",
    )(ids.reshape(1, T), rates.T, skip, q, k, v, x, b, c, gate)


def solution(mesh):
    placed = (
        P("seq", "tp"),
        P("seq", "tp"),
        P("seq", "tp"),
        P("seq", "tp"),
        P("seq", None),
        P("seq", "tp"),
        P("seq", "tp"),
        P("seq", "tp"),
        P("tp"),
        P("seq"),
    )
    return jax.shard_map(
        shards,
        mesh=mesh,
        in_specs=placed,
        out_specs=(P("seq", "tp"), P(("seq", "tp"), None), P("seq", "tp")),
        check_vma=False,
    )
```

```python
import functools
import math

import jax
import jax.numpy as jnp
from jax import lax
from jax.experimental import pallas as pl
from jax.experimental.pallas import tpu as pltpu
from jax.sharding import PartitionSpec as P

MESH = pl.DeviceIdType.MESH
F32 = jnp.float32
BF16 = jnp.bfloat16

T = 256
H = 8
D = 128
FEAT = 16
KROWS = D + FEAT
FAR = 16
HOPS = FAR // 2
CHUNK = 4
PIECES = 32
UNITS = 16
PER = UNITS // H
PAIR = 2
PROWS = D // PER
META = 3 * D
VMEM_LIMIT = 56 * 1024 * 1024
BIG = 1e30
LOG2E = math.log2(math.e)
SCALE2 = LOG2E / math.sqrt(D)


def dot(a, b):
    return lax.dot_general(a, b, (((1,), (0,)), ((), ())), preferred_element_type=F32)


def dot_t(a, b):
    return lax.dot_general(a, b, (((1,), (1,)), ((), ())), preferred_element_type=F32)


def head_lanes(h):
    return pl.ds(pl.multiple_of(h * D, D), D)


def wide(a, n):
    return jnp.concatenate([a] * n, axis=1)


def kernel(
    ids_ref,
    rates_ref,
    skip_ref,
    q_hbm,
    k_ref,
    v_ref,
    x_hbm,
    b_ref,
    c_hbm,
    gate_hbm,
    gx_ref,
    gb_ref,
    gc_ref,
    q_ref,
    x_ref,
    c_ref,
    gate_ref,
    own_k,
    own_v,
    far_k,
    far_v,
    qp,
    acc,
    top,
    log_row,
    log_col,
    mask,
    mask_t,
    decay,
    decay_t,
    mix_t,
    wc_t,
    b_t,
    ids_col,
    inner,
    g_ref,
    gx_part,
    h_term,
    meta,
    pass_up,
    pass_down,
    state_send,
    state_recv,
    entry_send,
    entry_recv,
    grad_send,
    grad_recv,
    exit_send,
    exit_recv,
    tp_send,
    tp_recv,
    far_send_sem,
    far_recv_sem,
    pass_send_sem,
    pass_recv_sem,
    pair_send_sem,
    pair_recv_sem,
    send_sem,
    recv_sem,
    unit_sem,
    load_sem,
):
    me = lax.axis_index("seq")
    z = lax.axis_index("tp")
    n_seq, n_tp = PIECES, 8

    base = jnp.where(me < 8, 0, jnp.where(me < 24, 8, 24))
    per = jnp.where((me >= 8) & (me < 24), 1, 2)
    count = jnp.where(per == 1, UNITS, UNITS // 2)
    base_in = jnp.where(me <= 8, 0, jnp.where(me <= 24, 8, 24))
    per_in = jnp.where((me > 8) & (me <= 24), 1, 2)

    chip = me // 2
    core = lax.rem(me, 2)
    n_out = jnp.where(chip < 4, 4 - chip, jnp.where(chip < 12, 12 - chip, 15 - chip))
    n_in = jnp.where(chip <= 4, chip, jnp.where(chip <= 12, chip - 4, chip - 12))

    low = jnp.where(chip <= 4, 0, jnp.where(chip <= 12, 8, 24))
    high = jnp.where(chip < 4, 9, jnp.where(chip < 12, 25, 31))

    barrier = pltpu.get_barrier_semaphore()

    def peer_at(k):
        return k + (k >= me).astype(jnp.int32)

    def greet_seq(k, carry):
        pl.semaphore_signal(
            barrier, inc=1, device_id=(peer_at(k), z), device_id_type=MESH
        )
        return carry

    def greet_tp(k, carry):
        pl.semaphore_signal(
            barrier, inc=1, device_id=(me, lax.rem(z + k, n_tp)), device_id_type=MESH
        )
        return carry

    lax.fori_loop(low, high, greet_seq, 0)
    lax.fori_loop(1, n_tp, greet_tp, 0)

    loads = [
        pltpu.make_async_copy(src, dst, load_sem.at[k])
        for k, (src, dst) in enumerate(
            ((x_hbm, x_ref), (c_hbm, c_ref), (q_hbm, q_ref), (gate_hbm, gate_ref))
        )
    ]
    for load in loads:
        load.start()

    ids_row = ids_ref[...].astype(F32)
    first_id = ids_row[:, 0:1]
    last_id = ids_row[:, T - 1 : T]
    feat_row = lax.broadcasted_iota(jnp.int32, (FEAT, T), 0).astype(F32)
    own_k[0:D, :] = k_ref[...].astype(F32).T.astype(BF16)
    own_k[D:KROWS, :] = jnp.where(
        feat_row == jnp.broadcast_to(ids_row, (FEAT, T)), 0.0, -BIG
    ).astype(BF16)
    own_k[KROWS:, :] = jnp.zeros((T - KROWS, T), BF16)
    own_v[:, 0:D] = v_ref[...]
    own_v[:, D:] = jnp.ones((T, D), BF16)

    pl.semaphore_wait(barrier, high - low + n_tp - 1)

    def block_copies(hop, which, src_k, src_v, peer, send_sems, recv_sems):
        at = pl.ds(pl.multiple_of((2 * hop + which) * T, T), T)
        return (
            pltpu.make_async_remote_copy(
                src_ref=src_k(at),
                dst_ref=far_k.at[0:D, at],
                send_sem=send_sems[0],
                recv_sem=recv_sems[0],
                device_id=(peer, z),
                device_id_type=MESH,
            ),
            pltpu.make_async_remote_copy(
                src_ref=src_v(at),
                dst_ref=far_v.at[at, 0:D],
                send_sem=send_sems[1],
                recv_sem=recv_sems[1],
                device_id=(peer, z),
                device_id_type=MESH,
            ),
        )

    sibling = me + 1 - 2 * core

    def own_block(at):
        return own_k.at[0:D, :]

    def own_values(at):
        return own_v.at[:, 0:D]

    def far_block(at):
        return far_k.at[0:D, at]

    def far_values(at):
        return far_v.at[at, 0:D]

    def far_copies(hop):
        peer = lax.rem(me + 2 + 2 * hop, n_seq)
        sends = (far_send_sem.at[0, hop], far_send_sem.at[1, hop])
        recvs = (far_recv_sem.at[0, hop], far_recv_sem.at[1, hop])
        return block_copies(hop, core, own_block, own_values, peer, sends, recvs)

    def pass_copies(hop, which):
        sends = (pass_send_sem.at[0, hop], pass_send_sem.at[1, hop])
        recvs = (pass_recv_sem.at[0, hop], pass_recv_sem.at[1, hop])
        return block_copies(hop, which, far_block, far_values, sibling, sends, recvs)

    def pair_copies():
        sends = (pair_send_sem.at[0], pair_send_sem.at[1])
        recvs = (pair_recv_sem.at[0], pair_recv_sem.at[1])
        return block_copies(HOPS - 1, 0, own_block, own_values, sibling, sends, recvs)

    def far_start(hop, carry):
        for copy in far_copies(hop):
            copy.start()
        return carry

    def passes(hop, which):
        return (hop < HOPS - 1) | (which == 1)

    def far_arrive(hop, carry):
        for copy in far_copies(hop):
            copy.wait_recv()

        @pl.when(passes(hop, core))
        def _():
            for copy in pass_copies(hop, core):
                copy.start()

        return carry

    def features(block, slot):
        at = pl.ds(pl.multiple_of(slot * T, T), T)
        far_k[D:KROWS, at] = jnp.where(
            feat_row == jnp.broadcast_to(meta[block][:, D:], (FEAT, T)), 0.0, -BIG
        ).astype(BF16)

    def pass_arrive(hop, carry):
        for which in range(2):
            features(jnp.maximum(me - core - 2 * hop - 2 + which, 0), 2 * hop + which)

        @pl.when(passes(hop, 1 - core))
        def _():
            for copy in pass_copies(hop, 1 - core):
                copy.wait_recv()

        return carry

    def hops(step, body):
        lax.fori_loop(
            jnp.minimum(n_in, 2 * step), jnp.minimum(n_in, 2 * step + 2), body, 0
        )

    @pl.when(core == 0)
    def _():
        for copy in pair_copies():
            copy.start()

    lax.fori_loop(0, n_out, far_start, 0)

    far_k[KROWS:, :] = jnp.zeros((T - KROWS, FAR * T), BF16)
    far_v[:, D:] = jnp.ones((FAR * T, D), BF16)

    def clear(j, carry):
        at = pl.ds(pl.multiple_of(j * T, T), T)

        @pl.when((core == 0) | (j != FAR - 2))
        def _():
            far_k[0:D, at] = jnp.zeros((D, T), BF16)
            far_k[D:KROWS, at] = jnp.full((FEAT, T), -BIG, BF16)
            far_v[at, 0:D] = jnp.zeros((T, D), BF16)

        return carry

    lax.fori_loop(2 * n_in, FAR, clear, 0)

    b_t[...] = b_ref[...].astype(F32).T.astype(BF16)
    idc = jnp.broadcast_to(ids_row, (D, T)).T
    ids_col[...] = idc

    row = lax.broadcasted_iota(jnp.int32, (T, T), 0)
    col = lax.broadcasted_iota(jnp.int32, (T, T), 1)
    log_row[...] = -LOG2E * lax.dot_general(
        rates_ref[...],
        (row <= col).astype(F32),
        (((1,), (0,)), ((), ())),
        precision=lax.Precision.HIGHEST,
        preferred_element_type=F32,
    )
    same = wide(idc, 2) == jnp.broadcast_to(ids_row, (T, T))
    mask[...] = jnp.where(same & (row >= col), 0.0, -BIG)
    mask_t[...] = jnp.where(same & (row <= col), 0.0, -BIG)

    end_bias = jnp.where(ids_row == last_id, 0.0, -BIG)
    whole = jnp.where(first_id == last_id, 1.0, 0.0)

    head_lane = lax.broadcasted_iota(jnp.int32, (H, D), 1)
    own_head = lax.broadcasted_iota(jnp.int32, (H, D), 0)
    ends = jnp.broadcast_to(jnp.exp2(log_row[:, T - 1 : T]) * whole, (H, D))
    ends = jnp.sum(jnp.where(head_lane == own_head, ends, 0.0), axis=0, keepdims=True)
    ends = jnp.where(head_lane[0:1, :] == H, first_id, ends)
    ends = jnp.where(head_lane[0:1, :] == H + 1, last_id, ends)
    meta[me] = jnp.concatenate([ends, ids_row], axis=1)

    def tell(k, carry):
        pltpu.make_async_remote_copy(
            src_ref=meta.at[me],
            dst_ref=meta.at[me],
            send_sem=send_sem.at[5],
            recv_sem=recv_sem.at[5],
            device_id=(peer_at(k), z),
            device_id_type=MESH,
        ).start()
        return carry

    def unheard(k, carry):
        @pl.when((k < low) | (k > high))
        def _():
            meta[k] = jnp.zeros((1, META), F32)

        return carry

    lax.fori_loop(low, high, tell, 0)
    lax.fori_loop(0, n_seq, unheard, 0)

    def states(h, carry):
        lr = log_row[pl.ds(h, 1), :]
        lend = lr[:, T - 1 : T]
        weight = jnp.exp2(lend - lr + end_bias)
        wt = (b_t[...].astype(F32) * jnp.broadcast_to(weight, (D, T))).astype(BF16)
        st = dot(wt, x_ref[:, head_lanes(h)]).astype(BF16)
        for p in range(PER):
            state_send[h * PER + p] = st[p * PROWS : (p + 1) * PROWS, :]
        return carry

    loads[0].wait()
    lax.fori_loop(0, H, states, 0)

    def unit_copy(source, target, phase, at, to, peer):
        return pltpu.make_async_remote_copy(
            src_ref=source.at[at],
            dst_ref=target.at[to],
            send_sem=send_sem.at[phase],
            recv_sem=unit_sem.at[phase, to],
            device_id=(peer, z),
            device_id_type=MESH,
        )

    def unit_send(source, target, phase, at, to, peer):
        @pl.when(peer != me)
        def _():
            unit_copy(source, target, phase, at, to, peer).start()

        @pl.when(peer == me)
        def _():
            target[to] = source[at]

    def unit_arrived(target, phase, to, peer):
        @pl.when(peer != me)
        def _():
            unit_copy(target, target, phase, to, to, peer).wait_recv()

    def wait_all(ref, sem, n, choices):
        for choice in choices:

            @pl.when(n == choice)
            def _(choice=choice):
                part = ref.at[pl.ds(0, choice)]
                pltpu.make_async_copy(part, part, sem).wait()

    def state_out(u, carry):
        k = jnp.where(per == 1, 0, lax.rem(u, 2))
        to = (me - base) * per + k
        unit_send(state_send, state_recv, 0, u, to, base + jnp.where(per == 1, u, u // 2))
        return carry

    lax.fori_loop(0, UNITS, state_out, 0)

    first_bias = jnp.where(ids_row == first_id, 0.0, -BIG)
    lane = lax.broadcasted_iota(jnp.int32, (T, D), 1).astype(F32)
    q_feat = jnp.where(lane == idc, 1.0, 0.0).astype(BF16)

    def local_head(h):
        lanes = head_lanes(h)
        lr = log_row[pl.ds(h, 1), :]
        lc = jnp.broadcast_to(lr, (D, T)).T
        lrb = jnp.broadcast_to(lr, (T, T))
        lcb = wide(lc, 2)
        ch = c_ref[:, lanes]
        ct = ch.astype(F32).T
        xh = x_ref[:, lanes]
        dec = jnp.exp2(lcb - lrb + mask[...])
        mix = (dot(ch, b_t[...]) * dec).astype(BF16)
        inn = dot(mix, xh) + skip_ref[h] * xh.astype(F32)
        dec_t = jnp.exp2(lrb - lcb + mask_t[...])
        mt = (dot(b_ref[...], ct.astype(BF16)) * dec_t).astype(BF16)
        wc = (ct * jnp.broadcast_to(jnp.exp2(lr + first_bias), (D, T))).astype(BF16)
        qh = jnp.concatenate([q_ref[:, lanes], q_feat], axis=1)
        s = jnp.where(row >= col, dot(qh, own_k[...]), -BIG)
        m = jnp.broadcast_to(jnp.max(s, axis=1, keepdims=True), (T, D))
        p = jnp.exp2((s - wide(m, 2)) * SCALE2)
        return lc, dec, inn, dec_t, mt, wc, qh, m, dot(p.astype(BF16), own_v[...])

    def local(i, carry):
        heads = [i * PAIR + k for k in range(PAIR)]
        done = [local_head(h) for h in heads]
        for h, (lc, dec, inn, dec_t, mt, wc, qh, m, o) in zip(heads, done):
            log_col[h] = lc
            decay[h] = dec
            inner[h] = inn
            decay_t[h] = dec_t
            mix_t[h] = mt
            wc_t[h] = wc
            rows = pl.ds(pl.multiple_of(h * T, T), T)
            qp[rows, :] = qh
            top[rows, :] = m
            acc[rows, :] = o
        return carry

    loads[1].wait()
    loads[2].wait()
    lax.fori_loop(0, H // PAIR // 2, local, 0)
    hops(0, far_arrive)
    lax.fori_loop(H // PAIR // 2, H // PAIR, local, 0)

    wait_all(meta, recv_sem.at[5], high - low, (7, 9, 17, 23, 25))
    lane_of = lax.broadcasted_iota(jnp.int32, (n_seq, D), 1)
    block_of = lax.broadcasted_iota(jnp.int32, (n_seq, D), 0)
    told = meta[...].reshape(n_seq, META)[:, 0:D]

    def lane_value(k):
        picked = jnp.sum(jnp.where(lane_of == k, told, 0.0), axis=1, keepdims=True)
        return jnp.broadcast_to(picked, (n_seq, D))

    thr = lane_value((me - base) * per // 2)
    firsts, lasts = lane_value(H), lane_value(H + 1)
    before = jnp.where(block_of == 0, -1.0, pltpu.roll(lasts, 1, 0))
    after = jnp.where(block_of == n_seq - 1, -1.0, pltpu.roll(firsts, n_seq - 1, 0))
    pass_up[...] = jnp.where(before == firsts, thr, 0.0)
    pass_down[...] = jnp.where(lasts == after, thr, 0.0)
    last_in = jnp.sum(jnp.where(block_of == me, before, 0.0), axis=0, keepdims=True)
    first_out = jnp.sum(jnp.where(block_of == me, after, 0.0), axis=0, keepdims=True)
    in_bias = jnp.where(idc == jnp.broadcast_to(last_in, (T, D)), 0.0, -BIG)
    out_bias = jnp.where(idc == jnp.broadcast_to(first_out, (T, D)), 0.0, -BIG)

    half = H * T // 2
    tile = half // 2

    def attend_rows(step, part):
        at = pl.ds(pl.multiple_of(step * CHUNK * T, CHUNK * T), CHUNK * T)
        tiles = [
            pl.ds(pl.multiple_of(part * half + k * tile, tile), tile) for k in range(2)
        ]
        scores = [dot(qp[r, :], far_k[:, at]) for r in tiles]
        weights = []
        for r, sc in zip(tiles, scores):
            old = top[r, :]
            new = jnp.maximum(
                old, jnp.broadcast_to(jnp.max(sc, axis=1, keepdims=True), (tile, D))
            )
            p = jnp.exp2((sc - wide(new, CHUNK * 2)) * SCALE2)
            weights.append((new, p.astype(BF16), jnp.exp2((old - new) * SCALE2)))
        sums = [
            acc[r, :] * wide(shrink, 2) + dot(p, far_v[at, :])
            for r, (new, p, shrink) in zip(tiles, weights)
        ]
        for r, (new, p, shrink), total in zip(tiles, weights, sums):
            top[r, :] = new
            acc[r, :] = total

    last_step = FAR // CHUNK - 1

    def attend(step, carry):
        @pl.when(n_in > 2 * step)
        def _():
            hops(step, pass_arrive)

            def rows_part(part, inner_carry):
                @pl.when(part == 1)
                def _():
                    hops(step + 1, far_arrive)

                attend_rows(step, part)
                return inner_carry

            lax.fori_loop(0, 2, rows_part, 0)

        return carry

    lax.fori_loop(0, 1, attend, 0)

    def forward(i, total):
        k = (i >= count).astype(jnp.int32)
        j = i - k * count
        slot = j * per + k
        c = base + j
        unit_arrived(state_recv, 0, slot, c)
        passing = jnp.where(j == 0, 0.0, pass_up[pl.ds(c, 1), :])
        total = jnp.broadcast_to(passing, (PROWS, D)) * total + state_recv[slot].astype(F32)
        entry_send[slot] = total.astype(BF16)

        @pl.when(c < n_seq - 1)
        def _():
            unit_send(entry_send, entry_recv, 1, slot, (me - base) * per + k, c + 1)

        return total

    lax.fori_loop(0, UNITS, forward, jnp.zeros((PROWS, D), F32))

    lax.fori_loop(1, last_step, attend, 0)

    def entry_in(u, carry):
        @pl.when(me > 0)
        def _():
            unit_arrived(entry_recv, 1, u, base_in + jnp.where(per_in == 1, u, u // 2))

        @pl.when(me == 0)
        def _():
            entry_recv[u] = jnp.zeros((PROWS, D), BF16)

        return carry

    lax.fori_loop(0, UNITS, entry_in, 0)

    def state_of(ref, h):
        parts = [ref[h * PER + p] for p in range(PER)]
        return jnp.concatenate(parts, axis=0)

    def student_head(h):
        lanes = head_lanes(h)
        carried = jnp.exp2(log_col[h] + in_bias)
        studied = inner[h] + dot(c_ref[:, lanes], state_of(entry_recv, h)) * carried
        gate = gate_ref[:, lanes].astype(F32)
        opened = gate / (1.0 + jnp.exp(-gate))
        return studied * opened * opened, opened

    def student(i, carry):
        heads = [i * PAIR + k for k in range(PAIR)]
        done = [student_head(h) for h in heads]
        for h, (ours, opened) in zip(heads, done):
            inner[h] = ours
            gx_part[h] = opened
        return carry

    loads[3].wait()
    lax.fori_loop(0, H // PAIR, student, 0)

    def mismatch_head(h):
        a = acc[pl.ds(pl.multiple_of(h * T, T), T), :]
        teacher = (a[:, 0:D] / a[:, D:]).astype(BF16).astype(F32)
        g = (inner[h] - teacher * gx_part[h]).astype(BF16)
        return g, dot(wc_t[h], g).astype(BF16)

    def mismatch(i, carry):
        heads = [i * PAIR + k for k in range(PAIR)]
        done = [mismatch_head(h) for h in heads]
        for h, (g, bg) in zip(heads, done):
            g_ref[h] = g
            for p in range(PER):
                grad_send[h * PER + p] = bg[p * PROWS : (p + 1) * PROWS, :]
        for u in [h * PER + p for h in heads for p in range(PER)]:

            @pl.when(me > 0)
            def _(u=u):
                k = jnp.where(per_in == 1, 0, lax.rem(u, 2))
                to = (me - 1 - base_in) * per_in + k
                peer = base_in + jnp.where(per_in == 1, u, u // 2)
                unit_send(grad_send, grad_recv, 2, u, to, peer)

        return carry

    @pl.when(n_in > 2 * last_step)
    def _():
        hops(last_step, pass_arrive)

    @pl.when(core == 1)
    def _():
        features(jnp.maximum(me - 1, 0), FAR - 2)
        for copy in pair_copies():
            copy.wait_recv()

    def last_part(part, carry):
        @pl.when((n_in > 2 * last_step) | (core == 1))
        def _():
            attend_rows(last_step, part)

        lax.fori_loop(part * (H // PAIR // 2), (part + 1) * (H // PAIR // 2), mismatch, 0)
        return carry

    lax.fori_loop(0, 2, last_part, 0)

    h_term[...] = jnp.zeros((T, D), F32)

    def within_head(h):
        lanes = head_lanes(h)
        g = g_ref[h]
        xh = x_ref[:, lanes]
        gx = dot(mix_t[h], g) + skip_ref[h] * g.astype(F32)
        gm = (dot_t(g, xh) * decay[h]).astype(BF16)
        carried = jnp.exp2(log_col[h] + in_bias)
        gc = dot(gm, b_ref[...]) + dot_t(g, state_of(entry_recv, h)) * carried
        gm_t = (dot_t(xh, g) * decay_t[h]).astype(BF16)
        return gx, gc.astype(BF16), dot(gm_t, c_ref[:, lanes])

    def within(i, carry):
        heads = [i * PAIR + k for k in range(PAIR)]
        done = [within_head(h) for h in heads]
        for h, (gx, gc, term) in zip(heads, done):
            gx_part[h] = gx
            gc_ref[:, head_lanes(h)] = gc
        h_term[...] += sum(term for gx, gc, term in done)
        return carry

    lax.fori_loop(0, H // PAIR // 2, within, 0)


    def reverse(i, total):
        k = (i >= count).astype(jnp.int32)
        j = count - 1 - (i - k * count)
        slot = j * per + k
        c = base + 1 + j

        @pl.when(c < n_seq)
        def _():
            unit_arrived(grad_recv, 2, slot, c)

        @pl.when(c == n_seq)
        def _():
            grad_recv[slot] = jnp.zeros((PROWS, D), BF16)

        row_of = pl.ds(jnp.minimum(c, n_seq - 1), 1)
        passing = jnp.where(j == count - 1, 0.0, pass_down[row_of, :])
        total = jnp.broadcast_to(passing, (PROWS, D)) * total + grad_recv[slot].astype(F32)
        exit_send[slot] = total.astype(BF16)
        unit_send(exit_send, exit_recv, 3, slot, (me - base) * per + k, base + j)
        return total

    lax.fori_loop(0, UNITS, reverse, jnp.zeros((PROWS, D), F32))

    lax.fori_loop(H // PAIR // 2, H // PAIR, within, 0)

    def exit_in(u, carry):
        unit_arrived(exit_recv, 3, u, base + jnp.where(per == 1, u, u // 2))
        return carry

    lax.fori_loop(0, UNITS, exit_in, 0)

    def next_decay(h):
        lc = log_col[h]
        return jnp.exp2(jnp.broadcast_to(lc[T - 1 : T, :], (T, D)) - lc + out_bias)

    def terms(i, carry):
        heads = [i * PAIR + k for k in range(PAIR)]
        h_term[...] += sum(
            dot_t(x_ref[:, head_lanes(h)], state_of(exit_recv, h)) * next_decay(h)
            for h in heads
        )
        return carry

    def finish(i, carry):
        heads = [i * PAIR + k for k in range(PAIR)]
        done = [
            (gx_part[h] + dot(b_ref[...], state_of(exit_recv, h)) * next_decay(h)).astype(BF16)
            for h in heads
        ]
        for h, gx in zip(heads, done):
            gx_ref[:, head_lanes(h)] = gx
        return carry

    lax.fori_loop(0, H // PAIR, terms, 0)

    rows = T // n_tp
    tp_send[...] = h_term[...].astype(BF16).reshape(n_tp, rows, D)

    def tp_copy(k, carry):
        peer = lax.rem(z + k, n_tp)
        pltpu.make_async_remote_copy(
            src_ref=tp_send.at[peer],
            dst_ref=tp_recv.at[z],
            send_sem=send_sem.at[4],
            recv_sem=recv_sem.at[4],
            device_id=(me, peer),
            device_id_type=MESH,
        ).start()
        return carry

    lax.fori_loop(1, n_tp, tp_copy, 0)
    tp_recv[z] = tp_send[z]
    lax.fori_loop(0, H // PAIR, finish, 0)
    rest = tp_recv.at[pl.ds(0, n_tp - 1)]
    pltpu.make_async_copy(rest, rest, recv_sem.at[4]).wait()
    total = jnp.zeros((rows, D), F32)
    for k in range(n_tp):
        total = total + tp_recv[k].astype(F32)
    gb_ref[...] = total.astype(BF16)

    first_of = (me == base).astype(jnp.int32)
    last_chain = (base == 24).astype(jnp.int32)
    no_worker = ((me == 8) | (me == 24)).astype(jnp.int32)
    sizes = (12, 14, 15, 16)
    wait_all(state_send, send_sem.at[0], UNITS - per, sizes)
    wait_all(entry_send, send_sem.at[1], UNITS - per * (1 - first_of + last_chain), sizes)
    wait_all(
        grad_send,
        send_sem.at[2],
        jnp.where(me == 0, 0, UNITS - per_in * (1 - no_worker)),
        sizes,
    )
    wait_all(exit_send, send_sem.at[3], UNITS - per, sizes)
    wait_all(meta, send_sem.at[5], high - low, (7, 9, 17, 23, 25))
    rest = tp_send.at[pl.ds(0, n_tp - 1)]
    pltpu.make_async_copy(rest, rest, send_sem.at[4]).wait()

    def far_left(hop, carry):
        for copy in far_copies(hop):
            copy.wait_send()
        return carry

    def pass_left(hop, carry):
        @pl.when(passes(hop, core))
        def _():
            for copy in pass_copies(hop, core):
                copy.wait_send()

        return carry

    lax.fori_loop(0, n_out, far_left, 0)
    lax.fori_loop(0, n_in, pass_left, 0)

    @pl.when(core == 0)
    def _():
        for copy in pair_copies():
            copy.wait_send()


def hand_over(gx_in, gb_in, gc_in, gx_out, gb_out, gc_out, gx, gb, gc, sem):
    ins = ((gx_in, gx), (gb_in, gb), (gc_in, gc))
    outs = ((gx, gx_out), (gb, gb_out), (gc, gc_out))
    get = [pltpu.make_async_copy(a, b, sem.at[k]) for k, (a, b) in enumerate(ins)]
    put = [pltpu.make_async_copy(a, b, sem.at[k]) for k, (a, b) in enumerate(outs)]
    for copy in get:
        copy.start()
    for first, second in zip(get, put):
        first.wait()
        second.start()
    for copy in put:
        copy.wait()


def shards(q, k, v, x, b, c, gate, rates, skip, ids):
    vmem = pl.BlockSpec(memory_space=pltpu.VMEM)
    smem = pl.BlockSpec(memory_space=pltpu.SMEM)
    anywhere = pl.BlockSpec(memory_space=pl.ANY)
    results = pl.pallas_call(
        kernel,
        out_shape=(
            jax.ShapeDtypeStruct((T, H * D), BF16),
            jax.ShapeDtypeStruct((T // 8, D), BF16),
            jax.ShapeDtypeStruct((T, H * D), BF16),
        ),
        in_specs=[vmem, vmem, smem, anywhere, vmem, vmem, anywhere, vmem, anywhere, anywhere],
        out_specs=(vmem, vmem, vmem),
        scratch_shapes=[
            pltpu.VMEM((T, H * D), BF16),
            pltpu.VMEM((T, H * D), BF16),
            pltpu.VMEM((T, H * D), BF16),
            pltpu.VMEM((T, H * D), BF16),
            pltpu.VMEM((T, T), BF16),
            pltpu.VMEM((T, T), BF16),
            pltpu.VMEM((T, FAR * T), BF16),
            pltpu.VMEM((FAR * T, T), BF16),
            pltpu.VMEM((H * T, T), BF16),
            pltpu.VMEM((H * T, T), F32),
            pltpu.VMEM((H * T, D), F32),
            pltpu.VMEM((H, T), F32),
            pltpu.VMEM((H, T, D), F32),
            pltpu.VMEM((T, T), F32),
            pltpu.VMEM((T, T), F32),
            pltpu.VMEM((H, T, T), F32),
            pltpu.VMEM((H, T, T), F32),
            pltpu.VMEM((H, T, T), BF16),
            pltpu.VMEM((H, D, T), BF16),
            pltpu.VMEM((D, T), BF16),
            pltpu.VMEM((T, D), F32),
            pltpu.VMEM((H, T, D), F32),
            pltpu.VMEM((H, T, D), BF16),
            pltpu.VMEM((H, T, D), F32),
            pltpu.VMEM((T, D), F32),
            pltpu.VMEM((PIECES, 1, META), F32),
            pltpu.VMEM((PIECES, D), F32),
            pltpu.VMEM((PIECES, D), F32),
            pltpu.VMEM((UNITS, PROWS, D), BF16),
            pltpu.VMEM((UNITS, PROWS, D), BF16),
            pltpu.VMEM((UNITS, PROWS, D), BF16),
            pltpu.VMEM((UNITS, PROWS, D), BF16),
            pltpu.VMEM((UNITS, PROWS, D), BF16),
            pltpu.VMEM((UNITS, PROWS, D), BF16),
            pltpu.VMEM((UNITS, PROWS, D), BF16),
            pltpu.VMEM((UNITS, PROWS, D), BF16),
            pltpu.VMEM((8, T // 8, D), BF16),
            pltpu.VMEM((8, T // 8, D), BF16),
            pltpu.SemaphoreType.DMA((2, HOPS)),
            pltpu.SemaphoreType.DMA((2, HOPS)),
            pltpu.SemaphoreType.DMA((2, HOPS)),
            pltpu.SemaphoreType.DMA((2, HOPS)),
            pltpu.SemaphoreType.DMA((2,)),
            pltpu.SemaphoreType.DMA((2,)),
            pltpu.SemaphoreType.DMA((6,)),
            pltpu.SemaphoreType.DMA((6,)),
            pltpu.SemaphoreType.DMA((4, UNITS)),
            pltpu.SemaphoreType.DMA((4,)),
        ],
        compiler_params=pltpu.CompilerParams(
            collective_id=0, has_side_effects=True, vmem_limit_bytes=VMEM_LIMIT
        ),
        name="distill",
    )(ids.reshape(1, T), rates.T, skip, q, k, v, x, b, c, gate)
    return pl.pallas_call(
        hand_over,
        out_shape=[jax.ShapeDtypeStruct(a.shape, a.dtype) for a in results],
        in_specs=[anywhere] * 3,
        out_specs=[anywhere] * 3,
        scratch_shapes=[pltpu.VMEM(a.shape, a.dtype) for a in results]
        + [pltpu.SemaphoreType.DMA((3,))],
        compiler_params=pltpu.CompilerParams(vmem_limit_bytes=60 * 1024 * 1024),
        name="hand_over",
    )(*results)


def solution(mesh):
    placed = (
        P("seq", "tp"),
        P("seq", "tp"),
        P("seq", "tp"),
        P("seq", "tp"),
        P("seq", None),
        P("seq", "tp"),
        P("seq", "tp"),
        P("seq", "tp"),
        P("tp"),
        P("seq"),
    )
    return jax.shard_map(
        shards,
        mesh=mesh,
        in_specs=placed,
        out_specs=(P("seq", "tp"), P(("seq", "tp"), None), P("seq", "tp")),
        check_vma=False,
    )
```

```python
import functools
import math

import jax
import jax.numpy as jnp
from jax import lax
from jax.experimental import pallas as pl
from jax.experimental.pallas import tpu as pltpu
from jax.sharding import PartitionSpec as P

MESH = pl.DeviceIdType.MESH
F32 = jnp.float32
BF16 = jnp.bfloat16

T = 256
H = 8
D = 128
FEAT = 16
KROWS = D + FEAT
FAR = 16
HOPS = FAR // 2
BELOW = 3
CHUNK = 4
PIECES = 32
UNITS = 16
PER = UNITS // H
PAIR = 4
PROWS = D // PER
META = 3 * D
VMEM_LIMIT = 56 * 1024 * 1024
BIG = 1e30
LOG2E = math.log2(math.e)
SCALE2 = LOG2E / math.sqrt(D)


def dot(a, b):
    return lax.dot_general(a, b, (((1,), (0,)), ((), ())), preferred_element_type=F32)


def dot_t(a, b):
    return lax.dot_general(a, b, (((1,), (1,)), ((), ())), preferred_element_type=F32)


def head_lanes(h):
    return pl.ds(pl.multiple_of(h * D, D), D)


def wide(a, n):
    return jnp.concatenate([a] * n, axis=1)


def kernel(
    ids_ref,
    rates_ref,
    skip_ref,
    q_hbm,
    k_ref,
    v_ref,
    x_hbm,
    b_ref,
    c_hbm,
    gate_hbm,
    gx_ref,
    gb_ref,
    gc_ref,
    q_ref,
    x_ref,
    c_ref,
    gate_ref,
    own_k,
    own_v,
    far_k,
    far_v,
    qp,
    acc,
    top,
    log_row,
    log_col,
    mask,
    mask_t,
    decay,
    decay_t,
    mix_t,
    wc_t,
    b_t,
    ids_col,
    inner,
    g_ref,
    gx_part,
    h_term,
    meta,
    pass_up,
    pass_down,
    state_send,
    state_recv,
    entry_send,
    entry_recv,
    grad_send,
    grad_recv,
    exit_send,
    exit_recv,
    tp_send,
    tp_recv,
    far_send_sem,
    far_recv_sem,
    pass_send_sem,
    pass_recv_sem,
    pair_send_sem,
    pair_recv_sem,
    relay_send_sem,
    send_sem,
    recv_sem,
    unit_sem,
    load_sem,
):
    me = lax.axis_index("seq")
    z = lax.axis_index("tp")
    n_seq, n_tp = PIECES, 8

    base = jnp.where(me < 8, 0, jnp.where(me < 24, 8, 24))
    per = jnp.where((me >= 8) & (me < 24), 1, 2)
    count = jnp.where(per == 1, UNITS, UNITS // 2)
    base_in = jnp.where(me <= 8, 0, jnp.where(me <= 24, 8, 24))
    per_in = jnp.where((me > 8) & (me <= 24), 1, 2)

    chip = me // 2
    core = lax.rem(me, 2)
    n_out = jnp.where(chip < 4, 4 - chip, jnp.where(chip < 12, 12 - chip, 15 - chip))
    n_in = jnp.where(chip <= 4, chip, jnp.where(chip <= 12, chip - 4, chip - 12))

    low = jnp.where(chip <= 4, 0, jnp.where(chip <= 12, 8, 24))
    high = jnp.where(chip < 4, 9, jnp.where(chip < 12, 25, 31))

    barrier = pltpu.get_barrier_semaphore()

    def peer_at(k):
        return k + (k >= me).astype(jnp.int32)

    def greet_seq(k, carry):
        pl.semaphore_signal(
            barrier, inc=1, device_id=(peer_at(k), z), device_id_type=MESH
        )
        return carry

    def greet_tp(k, carry):
        pl.semaphore_signal(
            barrier, inc=1, device_id=(me, lax.rem(z + k, n_tp)), device_id_type=MESH
        )
        return carry

    lax.fori_loop(low, high, greet_seq, 0)
    lax.fori_loop(1, n_tp, greet_tp, 0)

    loads = [
        pltpu.make_async_copy(src, dst, load_sem.at[k])
        for k, (src, dst) in enumerate(
            ((x_hbm, x_ref), (c_hbm, c_ref), (q_hbm, q_ref), (gate_hbm, gate_ref))
        )
    ]
    for load in loads:
        load.start()

    ids_row = ids_ref[...].astype(F32)
    first_id = ids_row[:, 0:1]
    last_id = ids_row[:, T - 1 : T]
    feat_row = lax.broadcasted_iota(jnp.int32, (FEAT, T), 0).astype(F32)
    own_k[0:D, :] = k_ref[...].astype(F32).T.astype(BF16)
    own_k[D:KROWS, :] = jnp.where(
        feat_row == jnp.broadcast_to(ids_row, (FEAT, T)), 0.0, -BIG
    ).astype(BF16)
    own_k[KROWS:, :] = jnp.zeros((T - KROWS, T), BF16)
    own_v[:, 0:D] = v_ref[...]
    own_v[:, D:] = jnp.ones((T, D), BF16)

    pl.semaphore_wait(barrier, high - low + n_tp - 1)

    def block_copies(hop, which, src_k, src_v, peer, send_sems, recv_sems):
        at = pl.ds(pl.multiple_of((2 * hop + which) * T, T), T)
        return (
            pltpu.make_async_remote_copy(
                src_ref=src_k(at),
                dst_ref=far_k.at[0:D, at],
                send_sem=send_sems[0],
                recv_sem=recv_sems[0],
                device_id=(peer, z),
                device_id_type=MESH,
            ),
            pltpu.make_async_remote_copy(
                src_ref=src_v(at),
                dst_ref=far_v.at[at, 0:D],
                send_sem=send_sems[1],
                recv_sem=recv_sems[1],
                device_id=(peer, z),
                device_id_type=MESH,
            ),
        )

    sibling = me + 1 - 2 * core

    def own_block(at):
        return own_k.at[0:D, :]

    def own_values(at):
        return own_v.at[:, 0:D]

    def far_block(at):
        return far_k.at[0:D, at]

    def far_values(at):
        return far_v.at[at, 0:D]

    def far_copies(hop):
        peer = lax.rem(me + 2 + 2 * hop, n_seq)
        sends = (far_send_sem.at[0, hop], far_send_sem.at[1, hop])
        recvs = (far_recv_sem.at[0, hop], far_recv_sem.at[1, hop])
        return block_copies(hop, core, own_block, own_values, peer, sends, recvs)

    def pass_copies(hop, which):
        sends = (pass_send_sem.at[0, hop], pass_send_sem.at[1, hop])
        recvs = (pass_recv_sem.at[0, hop], pass_recv_sem.at[1, hop])
        return block_copies(hop, which, far_block, far_values, sibling, sends, recvs)

    def pair_copies():
        sends = (pair_send_sem.at[0], pair_send_sem.at[1])
        recvs = (pair_recv_sem.at[0], pair_recv_sem.at[1])
        return block_copies(HOPS - 1, 0, own_block, own_values, sibling, sends, recvs)

    upper = (chip >= 4) & (chip < 8)
    lower = (chip >= 8) & (chip < 12)
    left_half = lax.rem(chip, 4) < 2
    across = jnp.where(left_half, BELOW + 2, BELOW - 2)

    def relay_copies():
        at = pl.ds(pl.multiple_of((2 * BELOW + core) * T, T), T)
        to = pl.ds(pl.multiple_of((2 * across + core) * T, T), T)
        peer = jnp.where(lower, me + 2 * (across - BELOW), sibling)
        pairs = (
            (far_k.at[0:D, at], far_k.at[0:D, to]),
            (far_v.at[at, 0:D], far_v.at[to, 0:D]),
        )
        return [
            pltpu.make_async_remote_copy(
                src_ref=src,
                dst_ref=dst,
                send_sem=relay_send_sem.at[k],
                recv_sem=far_recv_sem.at[k, across],
                device_id=(peer, z),
                device_id_type=MESH,
            )
            for k, (src, dst) in enumerate(pairs)
        ]

    def far_start(hop, carry):
        @pl.when(jnp.logical_not(upper & ((hop == across) | (hop == BELOW))))
        def _():
            for copy in far_copies(hop):
                copy.start()

        return carry

    def passes(hop, which):
        return (hop < HOPS - 1) | (which == 1)

    def far_take(hop):
        for copy in far_copies(hop):
            copy.wait_recv()

        @pl.when(passes(hop, core))
        def _():
            for copy in pass_copies(hop, core):
                copy.start()

    def far_arrive(hop, carry):
        @pl.when(jnp.logical_not(lower & (hop == BELOW)))
        def _():
            far_take(hop)

        return carry

    def features(block, slot):
        at = pl.ds(pl.multiple_of(slot * T, T), T)
        far_k[D:KROWS, at] = jnp.where(
            feat_row == jnp.broadcast_to(meta[block][:, D:], (FEAT, T)), 0.0, -BIG
        ).astype(BF16)

    def pass_arrive(hop, carry):
        for which in range(2):
            features(jnp.maximum(me - core - 2 * hop - 2 + which, 0), 2 * hop + which)

        @pl.when(passes(hop, 1 - core))
        def _():
            for copy in pass_copies(hop, 1 - core):
                copy.wait_recv()

        return carry

    def hops(step, body):
        lax.fori_loop(
            jnp.minimum(n_in, 2 * step), jnp.minimum(n_in, 2 * step + 2), body, 0
        )

    @pl.when(core == 0)
    def _():
        for copy in pair_copies():
            copy.start()

    @pl.when(upper)
    def _():
        for copy in far_copies(BELOW):
            copy.start()

    lax.fori_loop(0, n_out, far_start, 0)

    far_k[KROWS:, :] = jnp.zeros((T - KROWS, FAR * T), BF16)
    far_v[:, D:] = jnp.ones((FAR * T, D), BF16)

    def clear(j, carry):
        at = pl.ds(pl.multiple_of(j * T, T), T)

        @pl.when((core == 0) | (j != FAR - 2))
        def _():
            far_k[0:D, at] = jnp.zeros((D, T), BF16)
            far_k[D:KROWS, at] = jnp.full((FEAT, T), -BIG, BF16)
            far_v[at, 0:D] = jnp.zeros((T, D), BF16)

        return carry

    lax.fori_loop(2 * n_in, FAR, clear, 0)

    b_t[...] = b_ref[...].astype(F32).T.astype(BF16)
    idc = jnp.broadcast_to(ids_row, (D, T)).T
    ids_col[...] = idc

    row = lax.broadcasted_iota(jnp.int32, (T, T), 0)
    col = lax.broadcasted_iota(jnp.int32, (T, T), 1)
    log_row[...] = -LOG2E * lax.dot_general(
        rates_ref[...],
        (row <= col).astype(F32),
        (((1,), (0,)), ((), ())),
        precision=lax.Precision.HIGHEST,
        preferred_element_type=F32,
    )
    same = wide(idc, 2) == jnp.broadcast_to(ids_row, (T, T))
    mask[...] = jnp.where(same & (row >= col), 0.0, -BIG)
    mask_t[...] = jnp.where(same & (row <= col), 0.0, -BIG)

    end_bias = jnp.where(ids_row == last_id, 0.0, -BIG)
    whole = jnp.where(first_id == last_id, 1.0, 0.0)

    head_lane = lax.broadcasted_iota(jnp.int32, (H, D), 1)
    own_head = lax.broadcasted_iota(jnp.int32, (H, D), 0)
    ends = jnp.broadcast_to(jnp.exp2(log_row[:, T - 1 : T]) * whole, (H, D))
    ends = jnp.sum(jnp.where(head_lane == own_head, ends, 0.0), axis=0, keepdims=True)
    ends = jnp.where(head_lane[0:1, :] == H, first_id, ends)
    ends = jnp.where(head_lane[0:1, :] == H + 1, last_id, ends)
    meta[me] = jnp.concatenate([ends, ids_row], axis=1)

    def tell(k, carry):
        pltpu.make_async_remote_copy(
            src_ref=meta.at[me],
            dst_ref=meta.at[me],
            send_sem=send_sem.at[5],
            recv_sem=recv_sem.at[5],
            device_id=(peer_at(k), z),
            device_id_type=MESH,
        ).start()
        return carry

    def unheard(k, carry):
        @pl.when((k < low) | (k > high))
        def _():
            meta[k] = jnp.zeros((1, META), F32)

        return carry

    lax.fori_loop(low, high, tell, 0)
    lax.fori_loop(0, n_seq, unheard, 0)

    def states(h, carry):
        lr = log_row[pl.ds(h, 1), :]
        lend = lr[:, T - 1 : T]
        weight = jnp.exp2(lend - lr + end_bias)
        wt = (b_t[...].astype(F32) * jnp.broadcast_to(weight, (D, T))).astype(BF16)
        st = dot(wt, x_ref[:, head_lanes(h)]).astype(BF16)
        for p in range(PER):
            state_send[h * PER + p] = st[p * PROWS : (p + 1) * PROWS, :]
        return carry

    loads[0].wait()
    lax.fori_loop(0, H, states, 0)

    def unit_copy(source, target, phase, at, to, peer):
        return pltpu.make_async_remote_copy(
            src_ref=source.at[at],
            dst_ref=target.at[to],
            send_sem=send_sem.at[phase],
            recv_sem=unit_sem.at[phase, to],
            device_id=(peer, z),
            device_id_type=MESH,
        )

    def unit_send(source, target, phase, at, to, peer):
        @pl.when(peer != me)
        def _():
            unit_copy(source, target, phase, at, to, peer).start()

        @pl.when(peer == me)
        def _():
            target[to] = source[at]

    def unit_arrived(target, phase, to, peer):
        @pl.when(peer != me)
        def _():
            unit_copy(target, target, phase, to, to, peer).wait_recv()

    def wait_all(ref, sem, n, choices):
        for choice in choices:

            @pl.when(n == choice)
            def _(choice=choice):
                part = ref.at[pl.ds(0, choice)]
                pltpu.make_async_copy(part, part, sem).wait()

    def state_out(u, carry):
        k = jnp.where(per == 1, 0, lax.rem(u, 2))
        to = (me - base) * per + k
        unit_send(state_send, state_recv, 0, u, to, base + jnp.where(per == 1, u, u // 2))
        return carry

    lax.fori_loop(0, UNITS, state_out, 0)

    first_bias = jnp.where(ids_row == first_id, 0.0, -BIG)
    lane = lax.broadcasted_iota(jnp.int32, (T, D), 1).astype(F32)
    q_feat = jnp.where(lane == idc, 1.0, 0.0).astype(BF16)

    def local_head(h):
        lanes = head_lanes(h)
        lr = log_row[pl.ds(h, 1), :]
        lc = jnp.broadcast_to(lr, (D, T)).T
        lrb = jnp.broadcast_to(lr, (T, T))
        lcb = wide(lc, 2)
        ch = c_ref[:, lanes]
        ct = ch.astype(F32).T
        xh = x_ref[:, lanes]
        dec = jnp.exp2(lcb - lrb + mask[...])
        mix = (dot(ch, b_t[...]) * dec).astype(BF16)
        inn = dot(mix, xh) + skip_ref[h] * xh.astype(F32)
        dec_t = jnp.exp2(lrb - lcb + mask_t[...])
        mt = (dot(b_ref[...], ct.astype(BF16)) * dec_t).astype(BF16)
        wc = (ct * jnp.broadcast_to(jnp.exp2(lr + first_bias), (D, T))).astype(BF16)
        qh = jnp.concatenate([q_ref[:, lanes], q_feat], axis=1)
        s = jnp.where(row >= col, dot(qh, own_k[...]), -BIG)
        m = jnp.broadcast_to(jnp.max(s, axis=1, keepdims=True), (T, D))
        p = jnp.exp2((s - wide(m, 2)) * SCALE2)
        return lc, dec, inn, dec_t, mt, wc, qh, m, dot(p.astype(BF16), own_v[...])

    def local(i, carry):
        heads = [i * PAIR + k for k in range(PAIR)]
        done = [local_head(h) for h in heads]
        for h, (lc, dec, inn, dec_t, mt, wc, qh, m, o) in zip(heads, done):
            log_col[h] = lc
            decay[h] = dec
            inner[h] = inn
            decay_t[h] = dec_t
            mix_t[h] = mt
            wc_t[h] = wc
            rows = pl.ds(pl.multiple_of(h * T, T), T)
            qp[rows, :] = qh
            top[rows, :] = m
            acc[rows, :] = o
        return carry

    loads[1].wait()
    loads[2].wait()
    lax.fori_loop(0, H // PAIR // 2, local, 0)
    @pl.when(lower)
    def _():
        far_take(BELOW)
        for copy in relay_copies():
            copy.start()

    hops(0, far_arrive)
    lax.fori_loop(H // PAIR // 2, H // PAIR, local, 0)

    wait_all(meta, recv_sem.at[5], high - low, (7, 9, 17, 23, 25))
    lane_of = lax.broadcasted_iota(jnp.int32, (n_seq, D), 1)
    block_of = lax.broadcasted_iota(jnp.int32, (n_seq, D), 0)
    told = meta[...].reshape(n_seq, META)[:, 0:D]

    def lane_value(k):
        picked = jnp.sum(jnp.where(lane_of == k, told, 0.0), axis=1, keepdims=True)
        return jnp.broadcast_to(picked, (n_seq, D))

    thr = lane_value((me - base) * per // 2)
    firsts, lasts = lane_value(H), lane_value(H + 1)
    before = jnp.where(block_of == 0, -1.0, pltpu.roll(lasts, 1, 0))
    after = jnp.where(block_of == n_seq - 1, -1.0, pltpu.roll(firsts, n_seq - 1, 0))
    pass_up[...] = jnp.where(before == firsts, thr, 0.0)
    pass_down[...] = jnp.where(lasts == after, thr, 0.0)
    last_in = jnp.sum(jnp.where(block_of == me, before, 0.0), axis=0, keepdims=True)
    first_out = jnp.sum(jnp.where(block_of == me, after, 0.0), axis=0, keepdims=True)
    in_bias = jnp.where(idc == jnp.broadcast_to(last_in, (T, D)), 0.0, -BIG)
    out_bias = jnp.where(idc == jnp.broadcast_to(first_out, (T, D)), 0.0, -BIG)

    half = H * T // 2
    tile = half // 2

    def attend_rows(step, part):
        at = pl.ds(pl.multiple_of(step * CHUNK * T, CHUNK * T), CHUNK * T)
        tiles = [
            pl.ds(pl.multiple_of(part * half + k * tile, tile), tile) for k in range(2)
        ]
        scores = [dot(qp[r, :], far_k[:, at]) for r in tiles]
        weights = []
        for r, sc in zip(tiles, scores):
            old = top[r, :]
            new = jnp.maximum(
                old, jnp.broadcast_to(jnp.max(sc, axis=1, keepdims=True), (tile, D))
            )
            p = jnp.exp2((sc - wide(new, CHUNK * 2)) * SCALE2)
            weights.append((new, p.astype(BF16), jnp.exp2((old - new) * SCALE2)))
        sums = [
            acc[r, :] * wide(shrink, 2) + dot(p, far_v[at, :])
            for r, (new, p, shrink) in zip(tiles, weights)
        ]
        for r, (new, p, shrink), total in zip(tiles, weights, sums):
            top[r, :] = new
            acc[r, :] = total

    last_step = FAR // CHUNK - 1

    def attend(step, carry):
        @pl.when(n_in > 2 * step)
        def _():
            hops(step, pass_arrive)

            def rows_part(part, inner_carry):
                @pl.when(part == 1)
                def _():
                    hops(step + 1, far_arrive)

                attend_rows(step, part)
                return inner_carry

            lax.fori_loop(0, 2, rows_part, 0)

        return carry

    lax.fori_loop(0, 1, attend, 0)

    def forward(i, total):
        k = (i >= count).astype(jnp.int32)
        j = i - k * count
        slot = j * per + k
        c = base + j
        unit_arrived(state_recv, 0, slot, c)
        passing = jnp.where(j == 0, 0.0, pass_up[pl.ds(c, 1), :])
        total = jnp.broadcast_to(passing, (PROWS, D)) * total + state_recv[slot].astype(F32)
        entry_send[slot] = total.astype(BF16)

        @pl.when(c < n_seq - 1)
        def _():
            unit_send(entry_send, entry_recv, 1, slot, (me - base) * per + k, c + 1)

        return total

    lax.fori_loop(0, UNITS, forward, jnp.zeros((PROWS, D), F32))

    lax.fori_loop(1, last_step, attend, 0)

    def entry_in(u, carry):
        @pl.when(me > 0)
        def _():
            unit_arrived(entry_recv, 1, u, base_in + jnp.where(per_in == 1, u, u // 2))

        @pl.when(me == 0)
        def _():
            entry_recv[u] = jnp.zeros((PROWS, D), BF16)

        return carry

    lax.fori_loop(0, UNITS, entry_in, 0)

    def state_of(ref, h):
        parts = [ref[h * PER + p] for p in range(PER)]
        return jnp.concatenate(parts, axis=0)

    def student_head(h):
        lanes = head_lanes(h)
        carried = jnp.exp2(log_col[h] + in_bias)
        studied = inner[h] + dot(c_ref[:, lanes], state_of(entry_recv, h)) * carried
        gate = gate_ref[:, lanes].astype(F32)
        opened = gate / (1.0 + jnp.exp(-gate))
        return studied * opened * opened, opened

    def student(i, carry):
        heads = [i * PAIR + k for k in range(PAIR)]
        done = [student_head(h) for h in heads]
        for h, (ours, opened) in zip(heads, done):
            inner[h] = ours
            gx_part[h] = opened
        return carry

    loads[3].wait()
    lax.fori_loop(0, H // PAIR, student, 0)

    def mismatch_head(h):
        a = acc[pl.ds(pl.multiple_of(h * T, T), T), :]
        teacher = (a[:, 0:D] / a[:, D:]).astype(BF16).astype(F32)
        g = (inner[h] - teacher * gx_part[h]).astype(BF16)
        return g, dot(wc_t[h], g).astype(BF16)

    def mismatch(i, carry):
        heads = [i * PAIR + k for k in range(PAIR)]
        done = [mismatch_head(h) for h in heads]
        for h, (g, bg) in zip(heads, done):
            g_ref[h] = g
            for p in range(PER):
                grad_send[h * PER + p] = bg[p * PROWS : (p + 1) * PROWS, :]
        for u in [h * PER + p for h in heads for p in range(PER)]:

            @pl.when(me > 0)
            def _(u=u):
                k = jnp.where(per_in == 1, 0, lax.rem(u, 2))
                to = (me - 1 - base_in) * per_in + k
                peer = base_in + jnp.where(per_in == 1, u, u // 2)
                unit_send(grad_send, grad_recv, 2, u, to, peer)

        return carry

    @pl.when(n_in > 2 * last_step)
    def _():
        hops(last_step, pass_arrive)

    @pl.when(core == 1)
    def _():
        features(jnp.maximum(me - 1, 0), FAR - 2)
        for copy in pair_copies():
            copy.wait_recv()

    def last_part(part, carry):
        @pl.when((n_in > 2 * last_step) | (core == 1))
        def _():
            attend_rows(last_step, part)

        lax.fori_loop(part * (H // PAIR // 2), (part + 1) * (H // PAIR // 2), mismatch, 0)
        return carry

    lax.fori_loop(0, 2, last_part, 0)

    h_term[...] = jnp.zeros((T, D), F32)

    def within_head(h):
        lanes = head_lanes(h)
        g = g_ref[h]
        xh = x_ref[:, lanes]
        gx = dot(mix_t[h], g) + skip_ref[h] * g.astype(F32)
        gm = (dot_t(g, xh) * decay[h]).astype(BF16)
        carried = jnp.exp2(log_col[h] + in_bias)
        gc = dot(gm, b_ref[...]) + dot_t(g, state_of(entry_recv, h)) * carried
        gm_t = (dot_t(xh, g) * decay_t[h]).astype(BF16)
        return gx, gc.astype(BF16), dot(gm_t, c_ref[:, lanes])

    def within(i, carry):
        heads = [i * PAIR + k for k in range(PAIR)]
        done = [within_head(h) for h in heads]
        for h, (gx, gc, term) in zip(heads, done):
            gx_part[h] = gx
            gc_ref[:, head_lanes(h)] = gc
        h_term[...] += sum(term for gx, gc, term in done)
        return carry

    lax.fori_loop(0, H // PAIR // 2, within, 0)


    def reverse(i, total):
        k = (i >= count).astype(jnp.int32)
        j = count - 1 - (i - k * count)
        slot = j * per + k
        c = base + 1 + j

        @pl.when(c < n_seq)
        def _():
            unit_arrived(grad_recv, 2, slot, c)

        @pl.when(c == n_seq)
        def _():
            grad_recv[slot] = jnp.zeros((PROWS, D), BF16)

        row_of = pl.ds(jnp.minimum(c, n_seq - 1), 1)
        passing = jnp.where(j == count - 1, 0.0, pass_down[row_of, :])
        total = jnp.broadcast_to(passing, (PROWS, D)) * total + grad_recv[slot].astype(F32)
        exit_send[slot] = total.astype(BF16)
        unit_send(exit_send, exit_recv, 3, slot, (me - base) * per + k, base + j)
        return total

    lax.fori_loop(0, UNITS, reverse, jnp.zeros((PROWS, D), F32))

    lax.fori_loop(H // PAIR // 2, H // PAIR, within, 0)

    def exit_in(u, carry):
        unit_arrived(exit_recv, 3, u, base + jnp.where(per == 1, u, u // 2))
        return carry

    lax.fori_loop(0, UNITS, exit_in, 0)

    def next_decay(h):
        lc = log_col[h]
        return jnp.exp2(jnp.broadcast_to(lc[T - 1 : T, :], (T, D)) - lc + out_bias)

    def terms(i, carry):
        heads = [i * PAIR + k for k in range(PAIR)]
        h_term[...] += sum(
            dot_t(x_ref[:, head_lanes(h)], state_of(exit_recv, h)) * next_decay(h)
            for h in heads
        )
        return carry

    def finish(i, carry):
        heads = [i * PAIR + k for k in range(PAIR)]
        done = [
            (gx_part[h] + dot(b_ref[...], state_of(exit_recv, h)) * next_decay(h)).astype(BF16)
            for h in heads
        ]
        for h, gx in zip(heads, done):
            gx_ref[:, head_lanes(h)] = gx
        return carry

    lax.fori_loop(0, H // PAIR, terms, 0)

    rows = T // n_tp
    tp_send[...] = h_term[...].astype(BF16).reshape(n_tp, rows, D)

    def tp_copy(k, carry):
        peer = lax.rem(z + k, n_tp)
        pltpu.make_async_remote_copy(
            src_ref=tp_send.at[peer],
            dst_ref=tp_recv.at[z],
            send_sem=send_sem.at[4],
            recv_sem=recv_sem.at[4],
            device_id=(me, peer),
            device_id_type=MESH,
        ).start()
        return carry

    lax.fori_loop(1, n_tp, tp_copy, 0)
    tp_recv[z] = tp_send[z]
    lax.fori_loop(0, H // PAIR, finish, 0)
    rest = tp_recv.at[pl.ds(0, n_tp - 1)]
    pltpu.make_async_copy(rest, rest, recv_sem.at[4]).wait()
    total = jnp.zeros((rows, D), F32)
    for k in range(n_tp):
        total = total + tp_recv[k].astype(F32)
    gb_ref[...] = total.astype(BF16)

    first_of = (me == base).astype(jnp.int32)
    last_chain = (base == 24).astype(jnp.int32)
    no_worker = ((me == 8) | (me == 24)).astype(jnp.int32)
    sizes = (12, 14, 15, 16)
    wait_all(state_send, send_sem.at[0], UNITS - per, sizes)
    wait_all(entry_send, send_sem.at[1], UNITS - per * (1 - first_of + last_chain), sizes)
    wait_all(
        grad_send,
        send_sem.at[2],
        jnp.where(me == 0, 0, UNITS - per_in * (1 - no_worker)),
        sizes,
    )
    wait_all(exit_send, send_sem.at[3], UNITS - per, sizes)
    wait_all(meta, send_sem.at[5], high - low, (7, 9, 17, 23, 25))
    rest = tp_send.at[pl.ds(0, n_tp - 1)]
    pltpu.make_async_copy(rest, rest, send_sem.at[4]).wait()

    def far_left(hop, carry):
        @pl.when(jnp.logical_not(upper & (hop == across)))
        def _():
            for copy in far_copies(hop):
                copy.wait_send()

        return carry

    def pass_left(hop, carry):
        @pl.when(passes(hop, core))
        def _():
            for copy in pass_copies(hop, core):
                copy.wait_send()

        return carry

    lax.fori_loop(0, n_out, far_left, 0)

    @pl.when(lower)
    def _():
        for copy in relay_copies():
            copy.wait_send()

    lax.fori_loop(0, n_in, pass_left, 0)

    @pl.when(core == 0)
    def _():
        for copy in pair_copies():
            copy.wait_send()


def hand_over(gx_in, gb_in, gc_in, gx_out, gb_out, gc_out, gx, gb, gc, sem):
    ins = ((gx_in, gx), (gb_in, gb), (gc_in, gc))
    outs = ((gx, gx_out), (gb, gb_out), (gc, gc_out))
    get = [pltpu.make_async_copy(a, b, sem.at[k]) for k, (a, b) in enumerate(ins)]
    put = [pltpu.make_async_copy(a, b, sem.at[k]) for k, (a, b) in enumerate(outs)]
    for copy in get:
        copy.start()
    for first, second in zip(get, put):
        first.wait()
        second.start()
    for copy in put:
        copy.wait()


def shards(q, k, v, x, b, c, gate, rates, skip, ids):
    vmem = pl.BlockSpec(memory_space=pltpu.VMEM)
    smem = pl.BlockSpec(memory_space=pltpu.SMEM)
    anywhere = pl.BlockSpec(memory_space=pl.ANY)
    results = pl.pallas_call(
        kernel,
        out_shape=(
            jax.ShapeDtypeStruct((T, H * D), BF16),
            jax.ShapeDtypeStruct((T // 8, D), BF16),
            jax.ShapeDtypeStruct((T, H * D), BF16),
        ),
        in_specs=[vmem, vmem, smem, anywhere, vmem, vmem, anywhere, vmem, anywhere, anywhere],
        out_specs=(vmem, vmem, vmem),
        scratch_shapes=[
            pltpu.VMEM((T, H * D), BF16),
            pltpu.VMEM((T, H * D), BF16),
            pltpu.VMEM((T, H * D), BF16),
            pltpu.VMEM((T, H * D), BF16),
            pltpu.VMEM((T, T), BF16),
            pltpu.VMEM((T, T), BF16),
            pltpu.VMEM((T, FAR * T), BF16),
            pltpu.VMEM((FAR * T, T), BF16),
            pltpu.VMEM((H * T, T), BF16),
            pltpu.VMEM((H * T, T), F32),
            pltpu.VMEM((H * T, D), F32),
            pltpu.VMEM((H, T), F32),
            pltpu.VMEM((H, T, D), F32),
            pltpu.VMEM((T, T), F32),
            pltpu.VMEM((T, T), F32),
            pltpu.VMEM((H, T, T), F32),
            pltpu.VMEM((H, T, T), F32),
            pltpu.VMEM((H, T, T), BF16),
            pltpu.VMEM((H, D, T), BF16),
            pltpu.VMEM((D, T), BF16),
            pltpu.VMEM((T, D), F32),
            pltpu.VMEM((H, T, D), F32),
            pltpu.VMEM((H, T, D), BF16),
            pltpu.VMEM((H, T, D), F32),
            pltpu.VMEM((T, D), F32),
            pltpu.VMEM((PIECES, 1, META), F32),
            pltpu.VMEM((PIECES, D), F32),
            pltpu.VMEM((PIECES, D), F32),
            pltpu.VMEM((UNITS, PROWS, D), BF16),
            pltpu.VMEM((UNITS, PROWS, D), BF16),
            pltpu.VMEM((UNITS, PROWS, D), BF16),
            pltpu.VMEM((UNITS, PROWS, D), BF16),
            pltpu.VMEM((UNITS, PROWS, D), BF16),
            pltpu.VMEM((UNITS, PROWS, D), BF16),
            pltpu.VMEM((UNITS, PROWS, D), BF16),
            pltpu.VMEM((UNITS, PROWS, D), BF16),
            pltpu.VMEM((8, T // 8, D), BF16),
            pltpu.VMEM((8, T // 8, D), BF16),
            pltpu.SemaphoreType.DMA((2, HOPS)),
            pltpu.SemaphoreType.DMA((2, HOPS)),
            pltpu.SemaphoreType.DMA((2, HOPS)),
            pltpu.SemaphoreType.DMA((2, HOPS)),
            pltpu.SemaphoreType.DMA((2,)),
            pltpu.SemaphoreType.DMA((2,)),
            pltpu.SemaphoreType.DMA((2,)),
            pltpu.SemaphoreType.DMA((6,)),
            pltpu.SemaphoreType.DMA((6,)),
            pltpu.SemaphoreType.DMA((4, UNITS)),
            pltpu.SemaphoreType.DMA((4,)),
        ],
        compiler_params=pltpu.CompilerParams(
            collective_id=0, has_side_effects=True, vmem_limit_bytes=VMEM_LIMIT
        ),
        name="distill",
    )(ids.reshape(1, T), rates.T, skip, q, k, v, x, b, c, gate)
    return pl.pallas_call(
        hand_over,
        out_shape=[jax.ShapeDtypeStruct(a.shape, a.dtype) for a in results],
        in_specs=[anywhere] * 3,
        out_specs=[anywhere] * 3,
        scratch_shapes=[pltpu.VMEM(a.shape, a.dtype) for a in results]
        + [pltpu.SemaphoreType.DMA((3,))],
        compiler_params=pltpu.CompilerParams(vmem_limit_bytes=60 * 1024 * 1024),
        name="hand_over",
    )(*results)


def solution(mesh):
    placed = (
        P("seq", "tp"),
        P("seq", "tp"),
        P("seq", "tp"),
        P("seq", "tp"),
        P("seq", None),
        P("seq", "tp"),
        P("seq", "tp"),
        P("seq", "tp"),
        P("tp"),
        P("seq"),
    )
    return jax.shard_map(
        shards,
        mesh=mesh,
        in_specs=placed,
        out_specs=(P("seq", "tp"), P(("seq", "tp"), None), P("seq", "tp")),
        check_vma=False,
    )
```

```python
import functools
import math

import jax
import jax.numpy as jnp
from jax import lax
from jax.experimental import pallas as pl
from jax.experimental.pallas import tpu as pltpu
from jax.sharding import PartitionSpec as P

MESH = pl.DeviceIdType.MESH
F32 = jnp.float32
BF16 = jnp.bfloat16

T = 256
H = 8
D = 128
FEAT = 16
KROWS = D + FEAT
FAR = 16
HOPS = FAR // 2
BELOW = 3
CHUNK = 4
PIECES = 32
UNITS = 16
PER = UNITS // H
PAIR = 4
PROWS = D // PER
META = 3 * D
VMEM_LIMIT = 56 * 1024 * 1024
BIG = 1e30
LOG2E = math.log2(math.e)
SCALE2 = LOG2E / math.sqrt(D)


def dot(a, b):
    return lax.dot_general(a, b, (((1,), (0,)), ((), ())), preferred_element_type=F32)


def dot_t(a, b):
    return lax.dot_general(a, b, (((1,), (1,)), ((), ())), preferred_element_type=F32)


def head_lanes(h):
    return pl.ds(pl.multiple_of(h * D, D), D)


def wide(a, n):
    return jnp.concatenate([a] * n, axis=1)


def kernel(
    ids_ref,
    rates_ref,
    skip_ref,
    q_hbm,
    k_ref,
    v_ref,
    x_hbm,
    b_ref,
    c_hbm,
    gate_hbm,
    gx_hbm,
    gb_ref,
    gc_hbm,
    gx_ref,
    gc_ref,
    q_ref,
    x_ref,
    c_ref,
    gate_ref,
    own_k,
    own_v,
    far_k,
    far_v,
    qp,
    acc,
    top,
    log_row,
    log_col,
    mask,
    mask_t,
    decay,
    decay_t,
    mix_t,
    wc_t,
    b_t,
    ids_col,
    inner,
    g_ref,
    gx_part,
    h_term,
    meta,
    pass_up,
    pass_down,
    state_send,
    state_recv,
    entry_send,
    entry_recv,
    grad_send,
    grad_recv,
    exit_send,
    exit_recv,
    tp_send,
    tp_recv,
    far_send_sem,
    far_recv_sem,
    pass_send_sem,
    pass_recv_sem,
    pair_send_sem,
    pair_recv_sem,
    relay_send_sem,
    send_sem,
    recv_sem,
    unit_sem,
    load_sem,
    store_sem,
):
    me = lax.axis_index("seq")
    z = lax.axis_index("tp")
    n_seq, n_tp = PIECES, 8

    base = jnp.where(me < 8, 0, jnp.where(me < 24, 8, 24))
    per = jnp.where((me >= 8) & (me < 24), 1, 2)
    count = jnp.where(per == 1, UNITS, UNITS // 2)
    base_in = jnp.where(me <= 8, 0, jnp.where(me <= 24, 8, 24))
    per_in = jnp.where((me > 8) & (me <= 24), 1, 2)

    chip = me // 2
    core = lax.rem(me, 2)
    n_out = jnp.where(chip < 4, 4 - chip, jnp.where(chip < 12, 12 - chip, 15 - chip))
    n_in = jnp.where(chip <= 4, chip, jnp.where(chip <= 12, chip - 4, chip - 12))

    low = jnp.where(chip <= 4, 0, jnp.where(chip <= 12, 8, 24))
    high = jnp.where(chip < 4, 9, jnp.where(chip < 12, 25, 31))

    barrier = pltpu.get_barrier_semaphore()

    def peer_at(k):
        return k + (k >= me).astype(jnp.int32)

    def greet_seq(k, carry):
        pl.semaphore_signal(
            barrier, inc=1, device_id=(peer_at(k), z), device_id_type=MESH
        )
        return carry

    def greet_tp(k, carry):
        pl.semaphore_signal(
            barrier, inc=1, device_id=(me, lax.rem(z + k, n_tp)), device_id_type=MESH
        )
        return carry

    lax.fori_loop(low, high, greet_seq, 0)
    lax.fori_loop(1, n_tp, greet_tp, 0)

    loads = [
        pltpu.make_async_copy(src, dst, load_sem.at[k])
        for k, (src, dst) in enumerate(
            ((x_hbm, x_ref), (c_hbm, c_ref), (q_hbm, q_ref), (gate_hbm, gate_ref))
        )
    ]
    for load in loads:
        load.start()

    ids_row = ids_ref[...].astype(F32)
    first_id = ids_row[:, 0:1]
    last_id = ids_row[:, T - 1 : T]
    feat_row = lax.broadcasted_iota(jnp.int32, (FEAT, T), 0).astype(F32)
    own_k[0:D, :] = k_ref[...].astype(F32).T.astype(BF16)
    own_k[D:KROWS, :] = jnp.where(
        feat_row == jnp.broadcast_to(ids_row, (FEAT, T)), 0.0, -BIG
    ).astype(BF16)
    own_k[KROWS:, :] = jnp.zeros((T - KROWS, T), BF16)
    own_v[:, 0:D] = v_ref[...]
    own_v[:, D:] = jnp.ones((T, D), BF16)

    pl.semaphore_wait(barrier, high - low + n_tp - 1)

    def block_copies(hop, which, src_k, src_v, peer, send_sems, recv_sems):
        at = pl.ds(pl.multiple_of((2 * hop + which) * T, T), T)
        return (
            pltpu.make_async_remote_copy(
                src_ref=src_k(at),
                dst_ref=far_k.at[0:D, at],
                send_sem=send_sems[0],
                recv_sem=recv_sems[0],
                device_id=(peer, z),
                device_id_type=MESH,
            ),
            pltpu.make_async_remote_copy(
                src_ref=src_v(at),
                dst_ref=far_v.at[at, 0:D],
                send_sem=send_sems[1],
                recv_sem=recv_sems[1],
                device_id=(peer, z),
                device_id_type=MESH,
            ),
        )

    sibling = me + 1 - 2 * core

    def own_block(at):
        return own_k.at[0:D, :]

    def own_values(at):
        return own_v.at[:, 0:D]

    def far_block(at):
        return far_k.at[0:D, at]

    def far_values(at):
        return far_v.at[at, 0:D]

    def far_copies(hop):
        peer = lax.rem(me + 2 + 2 * hop, n_seq)
        sends = (far_send_sem.at[0, hop], far_send_sem.at[1, hop])
        recvs = (far_recv_sem.at[0, hop], far_recv_sem.at[1, hop])
        return block_copies(hop, core, own_block, own_values, peer, sends, recvs)

    def pass_copies(hop, which):
        sends = (pass_send_sem.at[0, hop], pass_send_sem.at[1, hop])
        recvs = (pass_recv_sem.at[0, hop], pass_recv_sem.at[1, hop])
        return block_copies(hop, which, far_block, far_values, sibling, sends, recvs)

    def pair_copies():
        sends = (pair_send_sem.at[0], pair_send_sem.at[1])
        recvs = (pair_recv_sem.at[0], pair_recv_sem.at[1])
        return block_copies(HOPS - 1, 0, own_block, own_values, sibling, sends, recvs)

    upper = (chip >= 4) & (chip < 8)
    lower = (chip >= 8) & (chip < 12)
    left_half = lax.rem(chip, 4) < 2
    across = jnp.where(left_half, BELOW + 2, BELOW - 2)

    def relay_copies():
        at = pl.ds(pl.multiple_of((2 * BELOW + core) * T, T), T)
        to = pl.ds(pl.multiple_of((2 * across + core) * T, T), T)
        peer = jnp.where(lower, me + 2 * (across - BELOW), sibling)
        pairs = (
            (far_k.at[0:D, at], far_k.at[0:D, to]),
            (far_v.at[at, 0:D], far_v.at[to, 0:D]),
        )
        return [
            pltpu.make_async_remote_copy(
                src_ref=src,
                dst_ref=dst,
                send_sem=relay_send_sem.at[k],
                recv_sem=far_recv_sem.at[k, across],
                device_id=(peer, z),
                device_id_type=MESH,
            )
            for k, (src, dst) in enumerate(pairs)
        ]

    def far_start(hop, carry):
        @pl.when(jnp.logical_not(upper & ((hop == across) | (hop == BELOW))))
        def _():
            for copy in far_copies(hop):
                copy.start()

        return carry

    def passes(hop, which):
        return (hop < HOPS - 1) | (which == 1)

    def far_take(hop):
        for copy in far_copies(hop):
            copy.wait_recv()

        @pl.when(passes(hop, core))
        def _():
            for copy in pass_copies(hop, core):
                copy.start()

    def far_arrive(hop, carry):
        @pl.when(jnp.logical_not(lower & (hop == BELOW)))
        def _():
            far_take(hop)

        return carry

    def features(block, slot):
        at = pl.ds(pl.multiple_of(slot * T, T), T)
        far_k[D:KROWS, at] = jnp.where(
            feat_row == jnp.broadcast_to(meta[block][:, D:], (FEAT, T)), 0.0, -BIG
        ).astype(BF16)

    def pass_arrive(hop, carry):
        for which in range(2):
            features(jnp.maximum(me - core - 2 * hop - 2 + which, 0), 2 * hop + which)

        @pl.when(passes(hop, 1 - core))
        def _():
            for copy in pass_copies(hop, 1 - core):
                copy.wait_recv()

        return carry

    def hops(step, body):
        lax.fori_loop(
            jnp.minimum(n_in, 2 * step), jnp.minimum(n_in, 2 * step + 2), body, 0
        )

    @pl.when(core == 0)
    def _():
        for copy in pair_copies():
            copy.start()

    @pl.when(upper)
    def _():
        for copy in far_copies(BELOW):
            copy.start()

    lax.fori_loop(0, n_out, far_start, 0)

    far_k[KROWS:, :] = jnp.zeros((T - KROWS, FAR * T), BF16)
    far_v[:, D:] = jnp.ones((FAR * T, D), BF16)

    def clear(j, carry):
        at = pl.ds(pl.multiple_of(j * T, T), T)

        @pl.when((core == 0) | (j != FAR - 2))
        def _():
            far_k[0:D, at] = jnp.zeros((D, T), BF16)
            far_k[D:KROWS, at] = jnp.full((FEAT, T), -BIG, BF16)
            far_v[at, 0:D] = jnp.zeros((T, D), BF16)

        return carry

    lax.fori_loop(2 * n_in, FAR, clear, 0)

    b_t[...] = b_ref[...].astype(F32).T.astype(BF16)
    idc = jnp.broadcast_to(ids_row, (D, T)).T
    ids_col[...] = idc

    row = lax.broadcasted_iota(jnp.int32, (T, T), 0)
    col = lax.broadcasted_iota(jnp.int32, (T, T), 1)
    log_row[...] = -LOG2E * lax.dot_general(
        rates_ref[...],
        (row <= col).astype(F32),
        (((1,), (0,)), ((), ())),
        precision=lax.Precision.HIGHEST,
        preferred_element_type=F32,
    )
    same = wide(idc, 2) == jnp.broadcast_to(ids_row, (T, T))
    mask[...] = jnp.where(same & (row >= col), 0.0, -BIG)
    mask_t[...] = jnp.where(same & (row <= col), 0.0, -BIG)

    end_bias = jnp.where(ids_row == last_id, 0.0, -BIG)
    whole = jnp.where(first_id == last_id, 1.0, 0.0)

    head_lane = lax.broadcasted_iota(jnp.int32, (H, D), 1)
    own_head = lax.broadcasted_iota(jnp.int32, (H, D), 0)
    ends = jnp.broadcast_to(jnp.exp2(log_row[:, T - 1 : T]) * whole, (H, D))
    ends = jnp.sum(jnp.where(head_lane == own_head, ends, 0.0), axis=0, keepdims=True)
    ends = jnp.where(head_lane[0:1, :] == H, first_id, ends)
    ends = jnp.where(head_lane[0:1, :] == H + 1, last_id, ends)
    meta[me] = jnp.concatenate([ends, ids_row], axis=1)

    def tell(k, carry):
        pltpu.make_async_remote_copy(
            src_ref=meta.at[me],
            dst_ref=meta.at[me],
            send_sem=send_sem.at[5],
            recv_sem=recv_sem.at[5],
            device_id=(peer_at(k), z),
            device_id_type=MESH,
        ).start()
        return carry

    def unheard(k, carry):
        @pl.when((k < low) | (k > high))
        def _():
            meta[k] = jnp.zeros((1, META), F32)

        return carry

    lax.fori_loop(low, high, tell, 0)
    lax.fori_loop(0, n_seq, unheard, 0)

    def states(h, carry):
        lr = log_row[pl.ds(h, 1), :]
        lend = lr[:, T - 1 : T]
        weight = jnp.exp2(lend - lr + end_bias)
        wt = (b_t[...].astype(F32) * jnp.broadcast_to(weight, (D, T))).astype(BF16)
        st = dot(wt, x_ref[:, head_lanes(h)]).astype(BF16)
        for p in range(PER):
            state_send[h * PER + p] = st[p * PROWS : (p + 1) * PROWS, :]
        return carry

    loads[0].wait()
    lax.fori_loop(0, H, states, 0)

    def unit_copy(source, target, phase, at, to, peer):
        return pltpu.make_async_remote_copy(
            src_ref=source.at[at],
            dst_ref=target.at[to],
            send_sem=send_sem.at[phase],
            recv_sem=unit_sem.at[phase, to],
            device_id=(peer, z),
            device_id_type=MESH,
        )

    def unit_send(source, target, phase, at, to, peer):
        @pl.when(peer != me)
        def _():
            unit_copy(source, target, phase, at, to, peer).start()

        @pl.when(peer == me)
        def _():
            target[to] = source[at]

    def unit_arrived(target, phase, to, peer):
        @pl.when(peer != me)
        def _():
            unit_copy(target, target, phase, to, to, peer).wait_recv()

    def wait_all(ref, sem, n, choices):
        for choice in choices:

            @pl.when(n == choice)
            def _(choice=choice):
                part = ref.at[pl.ds(0, choice)]
                pltpu.make_async_copy(part, part, sem).wait()

    def state_out(u, carry):
        k = jnp.where(per == 1, 0, lax.rem(u, 2))
        to = (me - base) * per + k
        unit_send(state_send, state_recv, 0, u, to, base + jnp.where(per == 1, u, u // 2))
        return carry

    lax.fori_loop(0, UNITS, state_out, 0)

    first_bias = jnp.where(ids_row == first_id, 0.0, -BIG)
    lane = lax.broadcasted_iota(jnp.int32, (T, D), 1).astype(F32)
    q_feat = jnp.where(lane == idc, 1.0, 0.0).astype(BF16)

    def local_head(h):
        lanes = head_lanes(h)
        lr = log_row[pl.ds(h, 1), :]
        lc = jnp.broadcast_to(lr, (D, T)).T
        lrb = jnp.broadcast_to(lr, (T, T))
        lcb = wide(lc, 2)
        ch = c_ref[:, lanes]
        ct = ch.astype(F32).T
        xh = x_ref[:, lanes]
        dec = jnp.exp2(lcb - lrb + mask[...])
        mix = (dot(ch, b_t[...]) * dec).astype(BF16)
        inn = dot(mix, xh) + skip_ref[h] * xh.astype(F32)
        dec_t = jnp.exp2(lrb - lcb + mask_t[...])
        mt = (dot(b_ref[...], ct.astype(BF16)) * dec_t).astype(BF16)
        wc = (ct * jnp.broadcast_to(jnp.exp2(lr + first_bias), (D, T))).astype(BF16)
        qh = jnp.concatenate([q_ref[:, lanes], q_feat], axis=1)
        s = jnp.where(row >= col, dot(qh, own_k[...]), -BIG)
        m = jnp.broadcast_to(jnp.max(s, axis=1, keepdims=True), (T, D))
        p = jnp.exp2((s - wide(m, 2)) * SCALE2)
        return lc, dec, inn, dec_t, mt, wc, qh, m, dot(p.astype(BF16), own_v[...])

    def local(i, carry):
        heads = [i * PAIR + k for k in range(PAIR)]
        done = [local_head(h) for h in heads]
        for h, (lc, dec, inn, dec_t, mt, wc, qh, m, o) in zip(heads, done):
            log_col[h] = lc
            decay[h] = dec
            inner[h] = inn
            decay_t[h] = dec_t
            mix_t[h] = mt
            wc_t[h] = wc
            rows = pl.ds(pl.multiple_of(h * T, T), T)
            qp[rows, :] = qh
            top[rows, :] = m
            acc[rows, :] = o
        return carry

    loads[1].wait()
    loads[2].wait()
    lax.fori_loop(0, H // PAIR // 2, local, 0)
    @pl.when(lower)
    def _():
        far_take(BELOW)
        for copy in relay_copies():
            copy.start()

    hops(0, far_arrive)
    lax.fori_loop(H // PAIR // 2, H // PAIR, local, 0)

    wait_all(meta, recv_sem.at[5], high - low, (7, 9, 17, 23, 25))
    lane_of = lax.broadcasted_iota(jnp.int32, (n_seq, D), 1)
    block_of = lax.broadcasted_iota(jnp.int32, (n_seq, D), 0)
    told = meta[...].reshape(n_seq, META)[:, 0:D]

    def lane_value(k):
        picked = jnp.sum(jnp.where(lane_of == k, told, 0.0), axis=1, keepdims=True)
        return jnp.broadcast_to(picked, (n_seq, D))

    thr = lane_value((me - base) * per // 2)
    firsts, lasts = lane_value(H), lane_value(H + 1)
    before = jnp.where(block_of == 0, -1.0, pltpu.roll(lasts, 1, 0))
    after = jnp.where(block_of == n_seq - 1, -1.0, pltpu.roll(firsts, n_seq - 1, 0))
    pass_up[...] = jnp.where(before == firsts, thr, 0.0)
    pass_down[...] = jnp.where(lasts == after, thr, 0.0)
    last_in = jnp.sum(jnp.where(block_of == me, before, 0.0), axis=0, keepdims=True)
    first_out = jnp.sum(jnp.where(block_of == me, after, 0.0), axis=0, keepdims=True)
    in_bias = jnp.where(idc == jnp.broadcast_to(last_in, (T, D)), 0.0, -BIG)
    out_bias = jnp.where(idc == jnp.broadcast_to(first_out, (T, D)), 0.0, -BIG)

    half = H * T // 2
    tile = half // 2

    def attend_rows(step, part):
        at = pl.ds(pl.multiple_of(step * CHUNK * T, CHUNK * T), CHUNK * T)
        tiles = [
            pl.ds(pl.multiple_of(part * half + k * tile, tile), tile) for k in range(2)
        ]
        scores = [dot(qp[r, :], far_k[:, at]) for r in tiles]
        weights = []
        for r, sc in zip(tiles, scores):
            old = top[r, :]
            new = jnp.maximum(
                old, jnp.broadcast_to(jnp.max(sc, axis=1, keepdims=True), (tile, D))
            )
            p = jnp.exp2((sc - wide(new, CHUNK * 2)) * SCALE2)
            weights.append((new, p.astype(BF16), jnp.exp2((old - new) * SCALE2)))
        sums = [
            acc[r, :] * wide(shrink, 2) + dot(p, far_v[at, :])
            for r, (new, p, shrink) in zip(tiles, weights)
        ]
        for r, (new, p, shrink), total in zip(tiles, weights, sums):
            top[r, :] = new
            acc[r, :] = total

    last_step = FAR // CHUNK - 1

    def attend(step, carry):
        @pl.when(n_in > 2 * step)
        def _():
            hops(step, pass_arrive)

            def rows_part(part, inner_carry):
                @pl.when(part == 1)
                def _():
                    hops(step + 1, far_arrive)

                attend_rows(step, part)
                return inner_carry

            lax.fori_loop(0, 2, rows_part, 0)

        return carry

    lax.fori_loop(0, 1, attend, 0)

    def forward(i, total):
        k = (i >= count).astype(jnp.int32)
        j = i - k * count
        slot = j * per + k
        c = base + j
        unit_arrived(state_recv, 0, slot, c)
        passing = jnp.where(j == 0, 0.0, pass_up[pl.ds(c, 1), :])
        total = jnp.broadcast_to(passing, (PROWS, D)) * total + state_recv[slot].astype(F32)
        entry_send[slot] = total.astype(BF16)

        @pl.when(c < n_seq - 1)
        def _():
            unit_send(entry_send, entry_recv, 1, slot, (me - base) * per + k, c + 1)

        return total

    lax.fori_loop(0, UNITS, forward, jnp.zeros((PROWS, D), F32))

    lax.fori_loop(1, last_step, attend, 0)

    def entry_in(u, carry):
        @pl.when(me > 0)
        def _():
            unit_arrived(entry_recv, 1, u, base_in + jnp.where(per_in == 1, u, u // 2))

        @pl.when(me == 0)
        def _():
            entry_recv[u] = jnp.zeros((PROWS, D), BF16)

        return carry

    lax.fori_loop(0, UNITS, entry_in, 0)

    def state_of(ref, h):
        parts = [ref[h * PER + p] for p in range(PER)]
        return jnp.concatenate(parts, axis=0)

    def student_head(h):
        lanes = head_lanes(h)
        carried = jnp.exp2(log_col[h] + in_bias)
        studied = inner[h] + dot(c_ref[:, lanes], state_of(entry_recv, h)) * carried
        gate = gate_ref[:, lanes].astype(F32)
        opened = gate / (1.0 + jnp.exp(-gate))
        return studied * opened * opened, opened

    def student(i, carry):
        heads = [i * PAIR + k for k in range(PAIR)]
        done = [student_head(h) for h in heads]
        for h, (ours, opened) in zip(heads, done):
            inner[h] = ours
            gx_part[h] = opened
        return carry

    loads[3].wait()
    lax.fori_loop(0, H // PAIR, student, 0)

    def mismatch_head(h):
        a = acc[pl.ds(pl.multiple_of(h * T, T), T), :]
        teacher = (a[:, 0:D] / a[:, D:]).astype(BF16).astype(F32)
        g = (inner[h] - teacher * gx_part[h]).astype(BF16)
        return g, dot(wc_t[h], g).astype(BF16)

    def mismatch(i, carry):
        heads = [i * PAIR + k for k in range(PAIR)]
        done = [mismatch_head(h) for h in heads]
        for h, (g, bg) in zip(heads, done):
            g_ref[h] = g
            for p in range(PER):
                grad_send[h * PER + p] = bg[p * PROWS : (p + 1) * PROWS, :]
        for u in [h * PER + p for h in heads for p in range(PER)]:

            @pl.when(me > 0)
            def _(u=u):
                k = jnp.where(per_in == 1, 0, lax.rem(u, 2))
                to = (me - 1 - base_in) * per_in + k
                peer = base_in + jnp.where(per_in == 1, u, u // 2)
                unit_send(grad_send, grad_recv, 2, u, to, peer)

        return carry

    @pl.when(n_in > 2 * last_step)
    def _():
        hops(last_step, pass_arrive)

    @pl.when(core == 1)
    def _():
        features(jnp.maximum(me - 1, 0), FAR - 2)
        for copy in pair_copies():
            copy.wait_recv()

    def last_part(part, carry):
        @pl.when((n_in > 2 * last_step) | (core == 1))
        def _():
            attend_rows(last_step, part)

        lax.fori_loop(part * (H // PAIR // 2), (part + 1) * (H // PAIR // 2), mismatch, 0)
        return carry

    lax.fori_loop(0, 2, last_part, 0)

    h_term[...] = jnp.zeros((T, D), F32)

    def within_head(h):
        lanes = head_lanes(h)
        g = g_ref[h]
        xh = x_ref[:, lanes]
        gx = dot(mix_t[h], g) + skip_ref[h] * g.astype(F32)
        gm = (dot_t(g, xh) * decay[h]).astype(BF16)
        carried = jnp.exp2(log_col[h] + in_bias)
        gc = dot(gm, b_ref[...]) + dot_t(g, state_of(entry_recv, h)) * carried
        gm_t = (dot_t(xh, g) * decay_t[h]).astype(BF16)
        return gx, gc.astype(BF16), dot(gm_t, c_ref[:, lanes])

    def within(i, carry):
        heads = [i * PAIR + k for k in range(PAIR)]
        done = [within_head(h) for h in heads]
        for h, (gx, gc, term) in zip(heads, done):
            gx_part[h] = gx
            gc_ref[:, head_lanes(h)] = gc
        h_term[...] += sum(term for gx, gc, term in done)
        return carry

    lax.fori_loop(0, H // PAIR // 2, within, 0)


    def reverse(i, total):
        k = (i >= count).astype(jnp.int32)
        j = count - 1 - (i - k * count)
        slot = j * per + k
        c = base + 1 + j

        @pl.when(c < n_seq)
        def _():
            unit_arrived(grad_recv, 2, slot, c)

        @pl.when(c == n_seq)
        def _():
            grad_recv[slot] = jnp.zeros((PROWS, D), BF16)

        row_of = pl.ds(jnp.minimum(c, n_seq - 1), 1)
        passing = jnp.where(j == count - 1, 0.0, pass_down[row_of, :])
        total = jnp.broadcast_to(passing, (PROWS, D)) * total + grad_recv[slot].astype(F32)
        exit_send[slot] = total.astype(BF16)
        unit_send(exit_send, exit_recv, 3, slot, (me - base) * per + k, base + j)
        return total

    lax.fori_loop(0, UNITS, reverse, jnp.zeros((PROWS, D), F32))

    lax.fori_loop(H // PAIR // 2, H // PAIR, within, 0)
    store_c = pltpu.make_async_copy(gc_ref, gc_hbm, store_sem.at[0])
    store_c.start()

    def exit_in(u, carry):
        unit_arrived(exit_recv, 3, u, base + jnp.where(per == 1, u, u // 2))
        return carry

    lax.fori_loop(0, UNITS, exit_in, 0)

    def next_decay(h):
        lc = log_col[h]
        return jnp.exp2(jnp.broadcast_to(lc[T - 1 : T, :], (T, D)) - lc + out_bias)

    def terms(i, carry):
        heads = [i * PAIR + k for k in range(PAIR)]
        h_term[...] += sum(
            dot_t(x_ref[:, head_lanes(h)], state_of(exit_recv, h)) * next_decay(h)
            for h in heads
        )
        return carry

    def finish(i, carry):
        heads = [i * PAIR + k for k in range(PAIR)]
        done = [
            (gx_part[h] + dot(b_ref[...], state_of(exit_recv, h)) * next_decay(h)).astype(BF16)
            for h in heads
        ]
        for h, gx in zip(heads, done):
            gx_ref[:, head_lanes(h)] = gx
        return carry

    lax.fori_loop(0, H // PAIR, terms, 0)

    rows = T // n_tp
    tp_send[...] = h_term[...].astype(BF16).reshape(n_tp, rows, D)

    def tp_copy(k, carry):
        peer = lax.rem(z + k, n_tp)
        pltpu.make_async_remote_copy(
            src_ref=tp_send.at[peer],
            dst_ref=tp_recv.at[z],
            send_sem=send_sem.at[4],
            recv_sem=recv_sem.at[4],
            device_id=(me, peer),
            device_id_type=MESH,
        ).start()
        return carry

    lax.fori_loop(1, n_tp, tp_copy, 0)
    tp_recv[z] = tp_send[z]
    lax.fori_loop(0, H // PAIR, finish, 0)
    store_x = pltpu.make_async_copy(gx_ref, gx_hbm, store_sem.at[1])
    store_x.start()
    rest = tp_recv.at[pl.ds(0, n_tp - 1)]
    pltpu.make_async_copy(rest, rest, recv_sem.at[4]).wait()
    total = jnp.zeros((rows, D), F32)
    for k in range(n_tp):
        total = total + tp_recv[k].astype(F32)
    gb_ref[...] = total.astype(BF16)
    store_c.wait()
    store_x.wait()

    first_of = (me == base).astype(jnp.int32)
    last_chain = (base == 24).astype(jnp.int32)
    no_worker = ((me == 8) | (me == 24)).astype(jnp.int32)
    sizes = (12, 14, 15, 16)
    wait_all(state_send, send_sem.at[0], UNITS - per, sizes)
    wait_all(entry_send, send_sem.at[1], UNITS - per * (1 - first_of + last_chain), sizes)
    wait_all(
        grad_send,
        send_sem.at[2],
        jnp.where(me == 0, 0, UNITS - per_in * (1 - no_worker)),
        sizes,
    )
    wait_all(exit_send, send_sem.at[3], UNITS - per, sizes)
    wait_all(meta, send_sem.at[5], high - low, (7, 9, 17, 23, 25))
    rest = tp_send.at[pl.ds(0, n_tp - 1)]
    pltpu.make_async_copy(rest, rest, send_sem.at[4]).wait()

    def far_left(hop, carry):
        @pl.when(jnp.logical_not(upper & (hop == across)))
        def _():
            for copy in far_copies(hop):
                copy.wait_send()

        return carry

    def pass_left(hop, carry):
        @pl.when(passes(hop, core))
        def _():
            for copy in pass_copies(hop, core):
                copy.wait_send()

        return carry

    lax.fori_loop(0, n_out, far_left, 0)

    @pl.when(lower)
    def _():
        for copy in relay_copies():
            copy.wait_send()

    lax.fori_loop(0, n_in, pass_left, 0)

    @pl.when(core == 0)
    def _():
        for copy in pair_copies():
            copy.wait_send()


def hand_over(gx_in, gb_in, gc_in, gx_out, gb_out, gc_out, gx, gb, gc, sem):
    ins = ((gx_in, gx), (gb_in, gb), (gc_in, gc))
    outs = ((gx, gx_out), (gb, gb_out), (gc, gc_out))
    get = [pltpu.make_async_copy(a, b, sem.at[k]) for k, (a, b) in enumerate(ins)]
    put = [pltpu.make_async_copy(a, b, sem.at[k]) for k, (a, b) in enumerate(outs)]
    for copy in get:
        copy.start()
    for first, second in zip(get, put):
        first.wait()
        second.start()
    for copy in put:
        copy.wait()


def shards(q, k, v, x, b, c, gate, rates, skip, ids):
    vmem = pl.BlockSpec(memory_space=pltpu.VMEM)
    smem = pl.BlockSpec(memory_space=pltpu.SMEM)
    anywhere = pl.BlockSpec(memory_space=pl.ANY)
    results = pl.pallas_call(
        kernel,
        out_shape=(
            jax.ShapeDtypeStruct((T, H * D), BF16),
            jax.ShapeDtypeStruct((T // 8, D), BF16),
            jax.ShapeDtypeStruct((T, H * D), BF16),
        ),
        in_specs=[vmem, vmem, smem, anywhere, vmem, vmem, anywhere, vmem, anywhere, anywhere],
        out_specs=(anywhere, vmem, anywhere),
        scratch_shapes=[
            pltpu.VMEM((T, H * D), BF16),
            pltpu.VMEM((T, H * D), BF16),
            pltpu.VMEM((T, H * D), BF16),
            pltpu.VMEM((T, H * D), BF16),
            pltpu.VMEM((T, H * D), BF16),
            pltpu.VMEM((T, H * D), BF16),
            pltpu.VMEM((T, T), BF16),
            pltpu.VMEM((T, T), BF16),
            pltpu.VMEM((T, FAR * T), BF16),
            pltpu.VMEM((FAR * T, T), BF16),
            pltpu.VMEM((H * T, T), BF16),
            pltpu.VMEM((H * T, T), F32),
            pltpu.VMEM((H * T, D), F32),
            pltpu.VMEM((H, T), F32),
            pltpu.VMEM((H, T, D), F32),
            pltpu.VMEM((T, T), F32),
            pltpu.VMEM((T, T), F32),
            pltpu.VMEM((H, T, T), F32),
            pltpu.VMEM((H, T, T), F32),
            pltpu.VMEM((H, T, T), BF16),
            pltpu.VMEM((H, D, T), BF16),
            pltpu.VMEM((D, T), BF16),
            pltpu.VMEM((T, D), F32),
            pltpu.VMEM((H, T, D), F32),
            pltpu.VMEM((H, T, D), BF16),
            pltpu.VMEM((H, T, D), F32),
            pltpu.VMEM((T, D), F32),
            pltpu.VMEM((PIECES, 1, META), F32),
            pltpu.VMEM((PIECES, D), F32),
            pltpu.VMEM((PIECES, D), F32),
            pltpu.VMEM((UNITS, PROWS, D), BF16),
            pltpu.VMEM((UNITS, PROWS, D), BF16),
            pltpu.VMEM((UNITS, PROWS, D), BF16),
            pltpu.VMEM((UNITS, PROWS, D), BF16),
            pltpu.VMEM((UNITS, PROWS, D), BF16),
            pltpu.VMEM((UNITS, PROWS, D), BF16),
            pltpu.VMEM((UNITS, PROWS, D), BF16),
            pltpu.VMEM((UNITS, PROWS, D), BF16),
            pltpu.VMEM((8, T // 8, D), BF16),
            pltpu.VMEM((8, T // 8, D), BF16),
            pltpu.SemaphoreType.DMA((2, HOPS)),
            pltpu.SemaphoreType.DMA((2, HOPS)),
            pltpu.SemaphoreType.DMA((2, HOPS)),
            pltpu.SemaphoreType.DMA((2, HOPS)),
            pltpu.SemaphoreType.DMA((2,)),
            pltpu.SemaphoreType.DMA((2,)),
            pltpu.SemaphoreType.DMA((2,)),
            pltpu.SemaphoreType.DMA((6,)),
            pltpu.SemaphoreType.DMA((6,)),
            pltpu.SemaphoreType.DMA((4, UNITS)),
            pltpu.SemaphoreType.DMA((4,)),
            pltpu.SemaphoreType.DMA((2,)),
        ],
        compiler_params=pltpu.CompilerParams(
            collective_id=0, has_side_effects=True, vmem_limit_bytes=VMEM_LIMIT
        ),
        name="distill",
    )(ids.reshape(1, T), rates.T, skip, q, k, v, x, b, c, gate)
    return pl.pallas_call(
        hand_over,
        out_shape=[jax.ShapeDtypeStruct(a.shape, a.dtype) for a in results],
        in_specs=[anywhere] * 3,
        out_specs=[anywhere] * 3,
        scratch_shapes=[pltpu.VMEM(a.shape, a.dtype) for a in results]
        + [pltpu.SemaphoreType.DMA((3,))],
        compiler_params=pltpu.CompilerParams(vmem_limit_bytes=60 * 1024 * 1024),
        name="hand_over",
    )(*results)


def solution(mesh):
    placed = (
        P("seq", "tp"),
        P("seq", "tp"),
        P("seq", "tp"),
        P("seq", "tp"),
        P("seq", None),
        P("seq", "tp"),
        P("seq", "tp"),
        P("seq", "tp"),
        P("tp"),
        P("seq"),
    )
    return jax.shard_map(
        shards,
        mesh=mesh,
        in_specs=placed,
        out_specs=(P("seq", "tp"), P(("seq", "tp"), None), P("seq", "tp")),
        check_vma=False,
    )
```

```python
import functools
import math

import jax
import jax.numpy as jnp
from jax import lax
from jax.experimental import pallas as pl
from jax.experimental.pallas import tpu as pltpu
from jax.sharding import PartitionSpec as P

MESH = pl.DeviceIdType.MESH
F32 = jnp.float32
BF16 = jnp.bfloat16

T = 256
H = 8
D = 128
FEAT = 16
KROWS = D + FEAT
FAR = 16
HOPS = FAR // 2
BELOW = 3
CHUNK = 4
PIECES = 32
UNITS = 16
PER = UNITS // H
PAIR = 4
PROWS = D // PER
META = 3 * D
VMEM_LIMIT = 56 * 1024 * 1024
BIG = 1e30
LOG2E = math.log2(math.e)
SCALE2 = LOG2E / math.sqrt(D)


def dot(a, b):
    return lax.dot_general(a, b, (((1,), (0,)), ((), ())), preferred_element_type=F32)


def dot_t(a, b):
    return lax.dot_general(a, b, (((1,), (1,)), ((), ())), preferred_element_type=F32)


def head_lanes(h):
    return pl.ds(pl.multiple_of(h * D, D), D)


def wide(a, n):
    return jnp.concatenate([a] * n, axis=1)


def kernel(
    ids_ref,
    rates_ref,
    skip_ref,
    q_hbm,
    k_ref,
    v_ref,
    x_hbm,
    b_ref,
    c_hbm,
    gate_hbm,
    gx_hbm,
    gb_ref,
    gc_hbm,
    gx_ref,
    gc_ref,
    q_ref,
    x_ref,
    c_ref,
    gate_ref,
    own_k,
    own_v,
    far_k,
    far_v,
    qp,
    acc,
    top,
    log_row,
    log_col,
    mask,
    mask_t,
    decay,
    decay_t,
    mix_t,
    wc_t,
    b_t,
    ids_col,
    inner,
    g_ref,
    gx_part,
    h_term,
    meta,
    pass_up,
    pass_down,
    state_send,
    state_recv,
    entry_send,
    entry_recv,
    grad_send,
    grad_recv,
    exit_send,
    exit_recv,
    tp_send,
    tp_recv,
    far_send_sem,
    far_recv_sem,
    pass_send_sem,
    pass_recv_sem,
    pair_send_sem,
    pair_recv_sem,
    relay_send_sem,
    send_sem,
    recv_sem,
    unit_sem,
    load_sem,
    store_sem,
):
    me = lax.axis_index("seq")
    z = lax.axis_index("tp")
    n_seq, n_tp = PIECES, 8

    base = jnp.where(me < 8, 0, jnp.where(me < 24, 8, 24))
    per = jnp.where((me >= 8) & (me < 24), 1, 2)
    count = jnp.where(per == 1, UNITS, UNITS // 2)
    base_in = jnp.where(me <= 8, 0, jnp.where(me <= 24, 8, 24))
    per_in = jnp.where((me > 8) & (me <= 24), 1, 2)

    chip = me // 2
    core = lax.rem(me, 2)
    n_out = jnp.where(chip < 4, 4 - chip, jnp.where(chip < 12, 12 - chip, 15 - chip))
    n_in = jnp.where(chip <= 4, chip, jnp.where(chip <= 12, chip - 4, chip - 12))

    low = jnp.where(chip <= 4, 0, jnp.where(chip <= 12, 8, 24))
    high = jnp.where(chip < 4, 9, jnp.where(chip < 12, 25, 31))

    barrier = pltpu.get_barrier_semaphore()

    def peer_at(k):
        return k + (k >= me).astype(jnp.int32)

    def greet_seq(k, carry):
        peer = peer_at(jnp.where(chip == 4, low + high - 1 - k, k))
        pl.semaphore_signal(barrier, inc=1, device_id=(peer, z), device_id_type=MESH)
        return carry

    def greet_tp(k, carry):
        pl.semaphore_signal(
            barrier, inc=1, device_id=(me, lax.rem(z + k, n_tp)), device_id_type=MESH
        )
        return carry

    lax.fori_loop(low, high, greet_seq, 0)
    lax.fori_loop(1, n_tp, greet_tp, 0)

    loads = [
        pltpu.make_async_copy(src, dst, load_sem.at[k])
        for k, (src, dst) in enumerate(
            ((x_hbm, x_ref), (c_hbm, c_ref), (q_hbm, q_ref), (gate_hbm, gate_ref))
        )
    ]
    for load in loads:
        load.start()

    ids_row = ids_ref[...].astype(F32)
    first_id = ids_row[:, 0:1]
    last_id = ids_row[:, T - 1 : T]
    feat_row = lax.broadcasted_iota(jnp.int32, (FEAT, T), 0).astype(F32)
    own_k[0:D, :] = k_ref[...].astype(F32).T.astype(BF16)
    own_k[D:KROWS, :] = jnp.where(
        feat_row == jnp.broadcast_to(ids_row, (FEAT, T)), 0.0, -BIG
    ).astype(BF16)
    own_k[KROWS:, :] = jnp.zeros((T - KROWS, T), BF16)
    own_v[:, 0:D] = v_ref[...]
    own_v[:, D:] = jnp.ones((T, D), BF16)

    pl.semaphore_wait(barrier, high - low + n_tp - 1)

    def block_copies(hop, which, src_k, src_v, peer, send_sems, recv_sems):
        at = pl.ds(pl.multiple_of((2 * hop + which) * T, T), T)
        return (
            pltpu.make_async_remote_copy(
                src_ref=src_k(at),
                dst_ref=far_k.at[0:D, at],
                send_sem=send_sems[0],
                recv_sem=recv_sems[0],
                device_id=(peer, z),
                device_id_type=MESH,
            ),
            pltpu.make_async_remote_copy(
                src_ref=src_v(at),
                dst_ref=far_v.at[at, 0:D],
                send_sem=send_sems[1],
                recv_sem=recv_sems[1],
                device_id=(peer, z),
                device_id_type=MESH,
            ),
        )

    sibling = me + 1 - 2 * core

    def own_block(at):
        return own_k.at[0:D, :]

    def own_values(at):
        return own_v.at[:, 0:D]

    def far_block(at):
        return far_k.at[0:D, at]

    def far_values(at):
        return far_v.at[at, 0:D]

    def far_copies(hop):
        peer = lax.rem(me + 2 + 2 * hop, n_seq)
        sends = (far_send_sem.at[0, hop], far_send_sem.at[1, hop])
        recvs = (far_recv_sem.at[0, hop], far_recv_sem.at[1, hop])
        return block_copies(hop, core, own_block, own_values, peer, sends, recvs)

    def pass_copies(hop, which):
        sends = (pass_send_sem.at[0, hop], pass_send_sem.at[1, hop])
        recvs = (pass_recv_sem.at[0, hop], pass_recv_sem.at[1, hop])
        return block_copies(hop, which, far_block, far_values, sibling, sends, recvs)

    def pair_copies():
        sends = (pair_send_sem.at[0], pair_send_sem.at[1])
        recvs = (pair_recv_sem.at[0], pair_recv_sem.at[1])
        return block_copies(HOPS - 1, 0, own_block, own_values, sibling, sends, recvs)

    upper = (chip >= 4) & (chip < 8)
    lower = (chip >= 8) & (chip < 12)
    left_half = lax.rem(chip, 4) < 2
    across = jnp.where(left_half, BELOW + 2, BELOW - 2)

    def relay_copies():
        at = pl.ds(pl.multiple_of((2 * BELOW + core) * T, T), T)
        to = pl.ds(pl.multiple_of((2 * across + core) * T, T), T)
        peer = jnp.where(lower, me + 2 * (across - BELOW), sibling)
        pairs = (
            (far_k.at[0:D, at], far_k.at[0:D, to]),
            (far_v.at[at, 0:D], far_v.at[to, 0:D]),
        )
        return [
            pltpu.make_async_remote_copy(
                src_ref=src,
                dst_ref=dst,
                send_sem=relay_send_sem.at[k],
                recv_sem=far_recv_sem.at[k, across],
                device_id=(peer, z),
                device_id_type=MESH,
            )
            for k, (src, dst) in enumerate(pairs)
        ]

    def far_start(hop, carry):
        @pl.when(jnp.logical_not(upper & ((hop == across) | (hop == BELOW))))
        def _():
            for copy in far_copies(hop):
                copy.start()

        return carry

    def passes(hop, which):
        return (hop < HOPS - 1) | (which == 1)

    def far_take(hop):
        for copy in far_copies(hop):
            copy.wait_recv()

        @pl.when(passes(hop, core))
        def _():
            for copy in pass_copies(hop, core):
                copy.start()

    def far_arrive(hop, carry):
        @pl.when(jnp.logical_not(lower & (hop == BELOW)))
        def _():
            far_take(hop)

        return carry

    def features(block, slot):
        at = pl.ds(pl.multiple_of(slot * T, T), T)
        far_k[D:KROWS, at] = jnp.where(
            feat_row == jnp.broadcast_to(meta[block][:, D:], (FEAT, T)), 0.0, -BIG
        ).astype(BF16)

    def pass_arrive(hop, carry):
        for which in range(2):
            features(jnp.maximum(me - core - 2 * hop - 2 + which, 0), 2 * hop + which)

        @pl.when(passes(hop, 1 - core))
        def _():
            for copy in pass_copies(hop, 1 - core):
                copy.wait_recv()

        return carry

    def hops(step, body):
        lax.fori_loop(
            jnp.minimum(n_in, 2 * step), jnp.minimum(n_in, 2 * step + 2), body, 0
        )

    @pl.when(upper)
    def _():
        for copy in far_copies(BELOW):
            copy.start()

    lax.fori_loop(0, n_out, far_start, 0)

    @pl.when(core == 0)
    def _():
        for copy in pair_copies():
            copy.start()

    far_k[KROWS:, :] = jnp.zeros((T - KROWS, FAR * T), BF16)
    far_v[:, D:] = jnp.ones((FAR * T, D), BF16)

    def clear(j, carry):
        at = pl.ds(pl.multiple_of(j * T, T), T)

        @pl.when((core == 0) | (j != FAR - 2))
        def _():
            far_k[0:D, at] = jnp.zeros((D, T), BF16)
            far_k[D:KROWS, at] = jnp.full((FEAT, T), -BIG, BF16)
            far_v[at, 0:D] = jnp.zeros((T, D), BF16)

        return carry

    lax.fori_loop(2 * n_in, FAR, clear, 0)

    b_t[...] = b_ref[...].astype(F32).T.astype(BF16)
    idc = jnp.broadcast_to(ids_row, (D, T)).T
    ids_col[...] = idc

    row = lax.broadcasted_iota(jnp.int32, (T, T), 0)
    col = lax.broadcasted_iota(jnp.int32, (T, T), 1)
    log_row[...] = -LOG2E * lax.dot_general(
        rates_ref[...],
        (row <= col).astype(F32),
        (((1,), (0,)), ((), ())),
        precision=lax.Precision.HIGHEST,
        preferred_element_type=F32,
    )
    same = wide(idc, 2) == jnp.broadcast_to(ids_row, (T, T))
    mask[...] = jnp.where(same & (row >= col), 0.0, -BIG)
    mask_t[...] = jnp.where(same & (row <= col), 0.0, -BIG)

    end_bias = jnp.where(ids_row == last_id, 0.0, -BIG)
    whole = jnp.where(first_id == last_id, 1.0, 0.0)

    head_lane = lax.broadcasted_iota(jnp.int32, (H, D), 1)
    own_head = lax.broadcasted_iota(jnp.int32, (H, D), 0)
    ends = jnp.broadcast_to(jnp.exp2(log_row[:, T - 1 : T]) * whole, (H, D))
    ends = jnp.sum(jnp.where(head_lane == own_head, ends, 0.0), axis=0, keepdims=True)
    ends = jnp.where(head_lane[0:1, :] == H, first_id, ends)
    ends = jnp.where(head_lane[0:1, :] == H + 1, last_id, ends)
    meta[me] = jnp.concatenate([ends, ids_row], axis=1)

    def tell(k, carry):
        pltpu.make_async_remote_copy(
            src_ref=meta.at[me],
            dst_ref=meta.at[me],
            send_sem=send_sem.at[5],
            recv_sem=recv_sem.at[5],
            device_id=(peer_at(k), z),
            device_id_type=MESH,
        ).start()
        return carry

    def unheard(k, carry):
        @pl.when((k < low) | (k > high))
        def _():
            meta[k] = jnp.zeros((1, META), F32)

        return carry

    lax.fori_loop(low, high, tell, 0)
    lax.fori_loop(0, n_seq, unheard, 0)

    def states(h, carry):
        lr = log_row[pl.ds(h, 1), :]
        lend = lr[:, T - 1 : T]
        weight = jnp.exp2(lend - lr + end_bias)
        wt = (b_t[...].astype(F32) * jnp.broadcast_to(weight, (D, T))).astype(BF16)
        st = dot(wt, x_ref[:, head_lanes(h)]).astype(BF16)
        for p in range(PER):
            state_send[h * PER + p] = st[p * PROWS : (p + 1) * PROWS, :]
        return carry

    loads[0].wait()
    lax.fori_loop(0, H, states, 0)

    def unit_copy(source, target, phase, at, to, peer):
        return pltpu.make_async_remote_copy(
            src_ref=source.at[at],
            dst_ref=target.at[to],
            send_sem=send_sem.at[phase],
            recv_sem=unit_sem.at[phase, to],
            device_id=(peer, z),
            device_id_type=MESH,
        )

    def unit_send(source, target, phase, at, to, peer):
        @pl.when(peer != me)
        def _():
            unit_copy(source, target, phase, at, to, peer).start()

        @pl.when(peer == me)
        def _():
            target[to] = source[at]

    def unit_arrived(target, phase, to, peer):
        @pl.when(peer != me)
        def _():
            unit_copy(target, target, phase, to, to, peer).wait_recv()

    def wait_all(ref, sem, n, choices):
        for choice in choices:

            @pl.when(n == choice)
            def _(choice=choice):
                part = ref.at[pl.ds(0, choice)]
                pltpu.make_async_copy(part, part, sem).wait()

    def state_out(u, carry):
        k = jnp.where(per == 1, 0, lax.rem(u, 2))
        to = (me - base) * per + k
        unit_send(state_send, state_recv, 0, u, to, base + jnp.where(per == 1, u, u // 2))
        return carry

    lax.fori_loop(0, UNITS, state_out, 0)

    first_bias = jnp.where(ids_row == first_id, 0.0, -BIG)
    lane = lax.broadcasted_iota(jnp.int32, (T, D), 1).astype(F32)
    q_feat = jnp.where(lane == idc, 1.0, 0.0).astype(BF16)

    def local_head(h):
        lanes = head_lanes(h)
        lr = log_row[pl.ds(h, 1), :]
        lc = jnp.broadcast_to(lr, (D, T)).T
        lrb = jnp.broadcast_to(lr, (T, T))
        lcb = wide(lc, 2)
        ch = c_ref[:, lanes]
        ct = ch.astype(F32).T
        xh = x_ref[:, lanes]
        dec = jnp.exp2(lcb - lrb + mask[...])
        mix = (dot(ch, b_t[...]) * dec).astype(BF16)
        inn = dot(mix, xh) + skip_ref[h] * xh.astype(F32)
        dec_t = jnp.exp2(lrb - lcb + mask_t[...])
        mt = (dot(b_ref[...], ct.astype(BF16)) * dec_t).astype(BF16)
        wc = (ct * jnp.broadcast_to(jnp.exp2(lr + first_bias), (D, T))).astype(BF16)
        qh = jnp.concatenate([q_ref[:, lanes], q_feat], axis=1)
        s = jnp.where(row >= col, dot(qh, own_k[...]), -BIG)
        m = jnp.broadcast_to(jnp.max(s, axis=1, keepdims=True), (T, D))
        p = jnp.exp2((s - wide(m, 2)) * SCALE2)
        return lc, dec, inn, dec_t, mt, wc, qh, m, dot(p.astype(BF16), own_v[...])

    def local(i, carry):
        heads = [i * PAIR + k for k in range(PAIR)]
        done = [local_head(h) for h in heads]
        for h, (lc, dec, inn, dec_t, mt, wc, qh, m, o) in zip(heads, done):
            log_col[h] = lc
            decay[h] = dec
            inner[h] = inn
            decay_t[h] = dec_t
            mix_t[h] = mt
            wc_t[h] = wc
            rows = pl.ds(pl.multiple_of(h * T, T), T)
            qp[rows, :] = qh
            top[rows, :] = m
            acc[rows, :] = o
        return carry

    loads[1].wait()
    loads[2].wait()
    lax.fori_loop(0, H // PAIR // 2, local, 0)
    @pl.when(lower)
    def _():
        far_take(BELOW)
        for copy in relay_copies():
            copy.start()

    hops(0, far_arrive)
    lax.fori_loop(H // PAIR // 2, H // PAIR, local, 0)

    wait_all(meta, recv_sem.at[5], high - low, (7, 9, 17, 23, 25))
    lane_of = lax.broadcasted_iota(jnp.int32, (n_seq, D), 1)
    block_of = lax.broadcasted_iota(jnp.int32, (n_seq, D), 0)
    told = meta[...].reshape(n_seq, META)[:, 0:D]

    def lane_value(k):
        picked = jnp.sum(jnp.where(lane_of == k, told, 0.0), axis=1, keepdims=True)
        return jnp.broadcast_to(picked, (n_seq, D))

    thr = lane_value((me - base) * per // 2)
    firsts, lasts = lane_value(H), lane_value(H + 1)
    before = jnp.where(block_of == 0, -1.0, pltpu.roll(lasts, 1, 0))
    after = jnp.where(block_of == n_seq - 1, -1.0, pltpu.roll(firsts, n_seq - 1, 0))
    pass_up[...] = jnp.where(before == firsts, thr, 0.0)
    pass_down[...] = jnp.where(lasts == after, thr, 0.0)
    last_in = jnp.sum(jnp.where(block_of == me, before, 0.0), axis=0, keepdims=True)
    first_out = jnp.sum(jnp.where(block_of == me, after, 0.0), axis=0, keepdims=True)
    in_bias = jnp.where(idc == jnp.broadcast_to(last_in, (T, D)), 0.0, -BIG)
    out_bias = jnp.where(idc == jnp.broadcast_to(first_out, (T, D)), 0.0, -BIG)

    half = H * T // 2
    tile = half // 2

    def attend_rows(step, part):
        at = pl.ds(pl.multiple_of(step * CHUNK * T, CHUNK * T), CHUNK * T)
        tiles = [
            pl.ds(pl.multiple_of(part * half + k * tile, tile), tile) for k in range(2)
        ]
        scores = [dot(qp[r, :], far_k[:, at]) for r in tiles]
        weights = []
        for r, sc in zip(tiles, scores):
            old = top[r, :]
            new = jnp.maximum(
                old, jnp.broadcast_to(jnp.max(sc, axis=1, keepdims=True), (tile, D))
            )
            p = jnp.exp2((sc - wide(new, CHUNK * 2)) * SCALE2)
            weights.append((new, p.astype(BF16), jnp.exp2((old - new) * SCALE2)))
        sums = [
            acc[r, :] * wide(shrink, 2) + dot(p, far_v[at, :])
            for r, (new, p, shrink) in zip(tiles, weights)
        ]
        for r, (new, p, shrink), total in zip(tiles, weights, sums):
            top[r, :] = new
            acc[r, :] = total

    last_step = FAR // CHUNK - 1

    def attend(step, carry):
        @pl.when(n_in > 2 * step)
        def _():
            hops(step, pass_arrive)

            def rows_part(part, inner_carry):
                @pl.when(part == 1)
                def _():
                    hops(step + 1, far_arrive)

                attend_rows(step, part)
                return inner_carry

            lax.fori_loop(0, 2, rows_part, 0)

        return carry

    lax.fori_loop(0, 1, attend, 0)

    def forward(i, total):
        k = (i >= count).astype(jnp.int32)
        j = i - k * count
        slot = j * per + k
        c = base + j
        unit_arrived(state_recv, 0, slot, c)
        passing = jnp.where(j == 0, 0.0, pass_up[pl.ds(c, 1), :])
        total = jnp.broadcast_to(passing, (PROWS, D)) * total + state_recv[slot].astype(F32)
        entry_send[slot] = total.astype(BF16)

        @pl.when(c < n_seq - 1)
        def _():
            unit_send(entry_send, entry_recv, 1, slot, (me - base) * per + k, c + 1)

        return total

    lax.fori_loop(0, UNITS, forward, jnp.zeros((PROWS, D), F32))

    lax.fori_loop(1, last_step, attend, 0)

    def entry_in(u, carry):
        @pl.when(me > 0)
        def _():
            unit_arrived(entry_recv, 1, u, base_in + jnp.where(per_in == 1, u, u // 2))

        @pl.when(me == 0)
        def _():
            entry_recv[u] = jnp.zeros((PROWS, D), BF16)

        return carry

    lax.fori_loop(0, UNITS, entry_in, 0)

    def state_of(ref, h):
        parts = [ref[h * PER + p] for p in range(PER)]
        return jnp.concatenate(parts, axis=0)

    def student_head(h):
        lanes = head_lanes(h)
        carried = jnp.exp2(log_col[h] + in_bias)
        studied = inner[h] + dot(c_ref[:, lanes], state_of(entry_recv, h)) * carried
        gate = gate_ref[:, lanes].astype(F32)
        opened = gate / (1.0 + jnp.exp(-gate))
        return studied * opened * opened, opened

    def student(i, carry):
        heads = [i * PAIR + k for k in range(PAIR)]
        done = [student_head(h) for h in heads]
        for h, (ours, opened) in zip(heads, done):
            inner[h] = ours
            gx_part[h] = opened
        return carry

    loads[3].wait()
    lax.fori_loop(0, H // PAIR, student, 0)

    def mismatch_head(h):
        a = acc[pl.ds(pl.multiple_of(h * T, T), T), :]
        teacher = (a[:, 0:D] / a[:, D:]).astype(BF16).astype(F32)
        g = (inner[h] - teacher * gx_part[h]).astype(BF16)
        return g, dot(wc_t[h], g).astype(BF16)

    def mismatch(i, carry):
        heads = [i * PAIR + k for k in range(PAIR)]
        done = [mismatch_head(h) for h in heads]
        for h, (g, bg) in zip(heads, done):
            g_ref[h] = g
            for p in range(PER):
                grad_send[h * PER + p] = bg[p * PROWS : (p + 1) * PROWS, :]
        for u in [h * PER + p for h in heads for p in range(PER)]:

            @pl.when(me > 0)
            def _(u=u):
                k = jnp.where(per_in == 1, 0, lax.rem(u, 2))
                to = (me - 1 - base_in) * per_in + k
                peer = base_in + jnp.where(per_in == 1, u, u // 2)
                unit_send(grad_send, grad_recv, 2, u, to, peer)

        return carry

    @pl.when(n_in > 2 * last_step)
    def _():
        hops(last_step, pass_arrive)

    @pl.when(core == 1)
    def _():
        features(jnp.maximum(me - 1, 0), FAR - 2)
        for copy in pair_copies():
            copy.wait_recv()

    def last_part(part, carry):
        @pl.when((n_in > 2 * last_step) | (core == 1))
        def _():
            attend_rows(last_step, part)

        lax.fori_loop(part * (H // PAIR // 2), (part + 1) * (H // PAIR // 2), mismatch, 0)
        return carry

    lax.fori_loop(0, 2, last_part, 0)

    h_term[...] = jnp.zeros((T, D), F32)

    def within_head(h):
        lanes = head_lanes(h)
        g = g_ref[h]
        xh = x_ref[:, lanes]
        gx = dot(mix_t[h], g) + skip_ref[h] * g.astype(F32)
        gm = (dot_t(g, xh) * decay[h]).astype(BF16)
        carried = jnp.exp2(log_col[h] + in_bias)
        gc = dot(gm, b_ref[...]) + dot_t(g, state_of(entry_recv, h)) * carried
        gm_t = (dot_t(xh, g) * decay_t[h]).astype(BF16)
        return gx, gc.astype(BF16), dot(gm_t, c_ref[:, lanes])

    def within(i, carry):
        heads = [i * PAIR + k for k in range(PAIR)]
        done = [within_head(h) for h in heads]
        for h, (gx, gc, term) in zip(heads, done):
            gx_part[h] = gx
            gc_ref[:, head_lanes(h)] = gc
        h_term[...] += sum(term for gx, gc, term in done)
        return carry

    lax.fori_loop(0, H // PAIR // 2, within, 0)


    def reverse(i, total):
        k = (i >= count).astype(jnp.int32)
        j = count - 1 - (i - k * count)
        slot = j * per + k
        c = base + 1 + j

        @pl.when(c < n_seq)
        def _():
            unit_arrived(grad_recv, 2, slot, c)

        @pl.when(c == n_seq)
        def _():
            grad_recv[slot] = jnp.zeros((PROWS, D), BF16)

        row_of = pl.ds(jnp.minimum(c, n_seq - 1), 1)
        passing = jnp.where(j == count - 1, 0.0, pass_down[row_of, :])
        total = jnp.broadcast_to(passing, (PROWS, D)) * total + grad_recv[slot].astype(F32)
        exit_send[slot] = total.astype(BF16)
        unit_send(exit_send, exit_recv, 3, slot, (me - base) * per + k, base + j)
        return total

    lax.fori_loop(0, UNITS, reverse, jnp.zeros((PROWS, D), F32))

    lax.fori_loop(H // PAIR // 2, H // PAIR, within, 0)
    store_c = pltpu.make_async_copy(gc_ref, gc_hbm, store_sem.at[0])
    store_c.start()

    def exit_in(u, carry):
        unit_arrived(exit_recv, 3, u, base + jnp.where(per == 1, u, u // 2))
        return carry

    lax.fori_loop(0, UNITS, exit_in, 0)

    def next_decay(h):
        lc = log_col[h]
        return jnp.exp2(jnp.broadcast_to(lc[T - 1 : T, :], (T, D)) - lc + out_bias)

    def terms(i, carry):
        heads = [i * PAIR + k for k in range(PAIR)]
        h_term[...] += sum(
            dot_t(x_ref[:, head_lanes(h)], state_of(exit_recv, h)) * next_decay(h)
            for h in heads
        )
        return carry

    def finish(i, carry):
        heads = [i * PAIR + k for k in range(PAIR)]
        done = [
            (gx_part[h] + dot(b_ref[...], state_of(exit_recv, h)) * next_decay(h)).astype(BF16)
            for h in heads
        ]
        for h, gx in zip(heads, done):
            gx_ref[:, head_lanes(h)] = gx
        return carry

    lax.fori_loop(0, H // PAIR, terms, 0)

    rows = T // n_tp
    tp_send[...] = h_term[...].astype(BF16).reshape(n_tp, rows, D)

    def tp_copy(k, carry):
        peer = lax.rem(z + k, n_tp)
        pltpu.make_async_remote_copy(
            src_ref=tp_send.at[peer],
            dst_ref=tp_recv.at[z],
            send_sem=send_sem.at[4],
            recv_sem=recv_sem.at[4],
            device_id=(me, peer),
            device_id_type=MESH,
        ).start()
        return carry

    lax.fori_loop(1, n_tp, tp_copy, 0)
    tp_recv[z] = tp_send[z]
    lax.fori_loop(0, H // PAIR, finish, 0)
    store_x = pltpu.make_async_copy(gx_ref, gx_hbm, store_sem.at[1])
    store_x.start()
    rest = tp_recv.at[pl.ds(0, n_tp - 1)]
    pltpu.make_async_copy(rest, rest, recv_sem.at[4]).wait()
    total = jnp.zeros((rows, D), F32)
    for k in range(n_tp):
        total = total + tp_recv[k].astype(F32)
    gb_ref[...] = total.astype(BF16)
    store_c.wait()
    store_x.wait()

    first_of = (me == base).astype(jnp.int32)
    last_chain = (base == 24).astype(jnp.int32)
    no_worker = ((me == 8) | (me == 24)).astype(jnp.int32)
    sizes = (12, 14, 15, 16)
    wait_all(state_send, send_sem.at[0], UNITS - per, sizes)
    wait_all(entry_send, send_sem.at[1], UNITS - per * (1 - first_of + last_chain), sizes)
    wait_all(
        grad_send,
        send_sem.at[2],
        jnp.where(me == 0, 0, UNITS - per_in * (1 - no_worker)),
        sizes,
    )
    wait_all(exit_send, send_sem.at[3], UNITS - per, sizes)
    wait_all(meta, send_sem.at[5], high - low, (7, 9, 17, 23, 25))
    rest = tp_send.at[pl.ds(0, n_tp - 1)]
    pltpu.make_async_copy(rest, rest, send_sem.at[4]).wait()

    def far_left(hop, carry):
        @pl.when(jnp.logical_not(upper & (hop == across)))
        def _():
            for copy in far_copies(hop):
                copy.wait_send()

        return carry

    def pass_left(hop, carry):
        @pl.when(passes(hop, core))
        def _():
            for copy in pass_copies(hop, core):
                copy.wait_send()

        return carry

    lax.fori_loop(0, n_out, far_left, 0)

    @pl.when(lower)
    def _():
        for copy in relay_copies():
            copy.wait_send()

    lax.fori_loop(0, n_in, pass_left, 0)

    @pl.when(core == 0)
    def _():
        for copy in pair_copies():
            copy.wait_send()


def hand_over(gx_in, gb_in, gc_in, gx_out, gb_out, gc_out, gx, gb, gc, sem):
    ins = ((gx_in, gx), (gb_in, gb), (gc_in, gc))
    outs = ((gx, gx_out), (gb, gb_out), (gc, gc_out))
    get = [pltpu.make_async_copy(a, b, sem.at[k]) for k, (a, b) in enumerate(ins)]
    put = [pltpu.make_async_copy(a, b, sem.at[k]) for k, (a, b) in enumerate(outs)]
    for copy in get:
        copy.start()
    for first, second in zip(get, put):
        first.wait()
        second.start()
    for copy in put:
        copy.wait()


def shards(q, k, v, x, b, c, gate, rates, skip, ids):
    vmem = pl.BlockSpec(memory_space=pltpu.VMEM)
    smem = pl.BlockSpec(memory_space=pltpu.SMEM)
    anywhere = pl.BlockSpec(memory_space=pl.ANY)
    results = pl.pallas_call(
        kernel,
        out_shape=(
            jax.ShapeDtypeStruct((T, H * D), BF16),
            jax.ShapeDtypeStruct((T // 8, D), BF16),
            jax.ShapeDtypeStruct((T, H * D), BF16),
        ),
        in_specs=[vmem, vmem, smem, anywhere, vmem, vmem, anywhere, vmem, anywhere, anywhere],
        out_specs=(anywhere, vmem, anywhere),
        scratch_shapes=[
            pltpu.VMEM((T, H * D), BF16),
            pltpu.VMEM((T, H * D), BF16),
            pltpu.VMEM((T, H * D), BF16),
            pltpu.VMEM((T, H * D), BF16),
            pltpu.VMEM((T, H * D), BF16),
            pltpu.VMEM((T, H * D), BF16),
            pltpu.VMEM((T, T), BF16),
            pltpu.VMEM((T, T), BF16),
            pltpu.VMEM((T, FAR * T), BF16),
            pltpu.VMEM((FAR * T, T), BF16),
            pltpu.VMEM((H * T, T), BF16),
            pltpu.VMEM((H * T, T), F32),
            pltpu.VMEM((H * T, D), F32),
            pltpu.VMEM((H, T), F32),
            pltpu.VMEM((H, T, D), F32),
            pltpu.VMEM((T, T), F32),
            pltpu.VMEM((T, T), F32),
            pltpu.VMEM((H, T, T), F32),
            pltpu.VMEM((H, T, T), F32),
            pltpu.VMEM((H, T, T), BF16),
            pltpu.VMEM((H, D, T), BF16),
            pltpu.VMEM((D, T), BF16),
            pltpu.VMEM((T, D), F32),
            pltpu.VMEM((H, T, D), F32),
            pltpu.VMEM((H, T, D), BF16),
            pltpu.VMEM((H, T, D), F32),
            pltpu.VMEM((T, D), F32),
            pltpu.VMEM((PIECES, 1, META), F32),
            pltpu.VMEM((PIECES, D), F32),
            pltpu.VMEM((PIECES, D), F32),
            pltpu.VMEM((UNITS, PROWS, D), BF16),
            pltpu.VMEM((UNITS, PROWS, D), BF16),
            pltpu.VMEM((UNITS, PROWS, D), BF16),
            pltpu.VMEM((UNITS, PROWS, D), BF16),
            pltpu.VMEM((UNITS, PROWS, D), BF16),
            pltpu.VMEM((UNITS, PROWS, D), BF16),
            pltpu.VMEM((UNITS, PROWS, D), BF16),
            pltpu.VMEM((UNITS, PROWS, D), BF16),
            pltpu.VMEM((8, T // 8, D), BF16),
            pltpu.VMEM((8, T // 8, D), BF16),
            pltpu.SemaphoreType.DMA((2, HOPS)),
            pltpu.SemaphoreType.DMA((2, HOPS)),
            pltpu.SemaphoreType.DMA((2, HOPS)),
            pltpu.SemaphoreType.DMA((2, HOPS)),
            pltpu.SemaphoreType.DMA((2,)),
            pltpu.SemaphoreType.DMA((2,)),
            pltpu.SemaphoreType.DMA((2,)),
            pltpu.SemaphoreType.DMA((6,)),
            pltpu.SemaphoreType.DMA((6,)),
            pltpu.SemaphoreType.DMA((4, UNITS)),
            pltpu.SemaphoreType.DMA((4,)),
            pltpu.SemaphoreType.DMA((2,)),
        ],
        compiler_params=pltpu.CompilerParams(
            collective_id=0, has_side_effects=True, vmem_limit_bytes=VMEM_LIMIT
        ),
        name="distill",
    )(ids.reshape(1, T), rates.T, skip, q, k, v, x, b, c, gate)
    return pl.pallas_call(
        hand_over,
        out_shape=[jax.ShapeDtypeStruct(a.shape, a.dtype) for a in results],
        in_specs=[anywhere] * 3,
        out_specs=[anywhere] * 3,
        scratch_shapes=[pltpu.VMEM(a.shape, a.dtype) for a in results]
        + [pltpu.SemaphoreType.DMA((3,))],
        compiler_params=pltpu.CompilerParams(vmem_limit_bytes=60 * 1024 * 1024),
        name="hand_over",
    )(*results)


def solution(mesh):
    placed = (
        P("seq", "tp"),
        P("seq", "tp"),
        P("seq", "tp"),
        P("seq", "tp"),
        P("seq", None),
        P("seq", "tp"),
        P("seq", "tp"),
        P("seq", "tp"),
        P("tp"),
        P("seq"),
    )
    return jax.shard_map(
        shards,
        mesh=mesh,
        in_specs=placed,
        out_specs=(P("seq", "tp"), P(("seq", "tp"), None), P("seq", "tp")),
        check_vma=False,
    )
```
